32 devices in a mesh: dp: 8 (over z, x), frame: 4 (over y, core).
Axes of the slice: x: 2, y: 2, z: 4, core: 2. Of those that a mesh axis runs over, the one named last changes fastest.
Arguments:
- hidden_in: bfloat16 [8192, 1280], P(('dp', 'frame')), may hold values from -6 to 6
- rec_lengths: int32 [8, 3], P('dp'), may hold values from 1 to 512, 1024 in all within a row
- token_positions: int32 [8192], P('dp'), may hold values from 0 to 1535, as said below
- thinker_grad: bfloat16 [12288, 1280], P(('dp', 'frame')), may hold values from -6 to 6
- norm_gain: float32 [1280], replicated, may hold values from 0.25 to 1.75
- norm_bias: float32 [1280], replicated, may hold values from -3 to 3
- qkv_weight: bfloat16 [1280, 3, 1280], P('dp', None, 'frame'), may hold values from -10 to 10
Outputs:
- hidden_grad: bfloat16 [8192, 1280], P(('dp', 'frame'))
- weight_grad: float32 [1280, 3, 1280], P('dp', None, 'frame')
The draws below stay inside these ranges and needn't reach their ends.
Inputs may be any that keep to these rules, and one draw needn't show every extreme that they name: `token_positions`: within each block of 1024 entries the positions increase strictly; the first is 0 and the last is 1535.
All inputs are finite; a program needn't handle non-finite values.
Results may differ from the reference program's by a relative error of at most 0.025.
The reference program's roundings to bfloat16 on the way (of `normalized`, `projected`, `out_grad`, `weights_low`, `score_grad` and `proj_grad`) count: a program that leaves them out, or rounds other values in their place, can miss the bound.
Values may be sent and summed in bfloat16 or wider, within the bound.
A program may use at most 128 MiB of HBM per device.

```python
import math
import jax
import jax.numpy as jnp
import numpy as np
from jax import lax

D = 1280
HEADS = 20
HD = 64
REC = 3
FRAMES_G = 1024
FRAMES = 8192
THINK_G = 1536
THINK_ALL = 12288
MOST = 512
GROUPS = 8


def draw_token_positions(key, part):
    groups = FRAMES // FRAMES_G
    group_keys = jax.random.split(key, groups)

    def one_group(group_key):
        middle = jax.random.permutation(group_key, THINK_G - 2).astype(jnp.int32) + 1
        chosen = jnp.sort(middle[:FRAMES_G - 2])
        return jnp.concatenate([jnp.zeros((1,), jnp.int32), chosen, jnp.full((1,), THINK_G - 1, jnp.int32)])
    return jax.vmap(one_group)(group_keys).reshape(FRAMES)


def draw_qkv_weight(key, part):
    base_key = jax.random.fold_in(jax.random.fold_in(key, 17), 0)
    base = jnp.clip(jax.random.normal(base_key, (D, 3, D), jnp.float32), -4.0, 4.0) * D ** (-0.5)
    return base.astype(jnp.bfloat16)


def with_spikes(drawn, stream_key, source, target, blocks, factor):
    owner, partner = [(jnp.arange(drawn.shape[dim]) // (drawn.shape[dim] // blocks)).reshape([-1 if axis == dim else 1 for axis in range(drawn.ndim)]) for dim in (source, target)]
    chosen = jax.random.permutation(stream_key, blocks)[partner]
    strong = (owner == chosen) | (owner == (partner + blocks // 2) % blocks)
    return jnp.where(strong, factor * drawn, drawn)


def block_levels(own_key, extent, cuts, low, largest):
    def one(axis_at, blocks):
        draws = jax.random.uniform(jax.random.fold_in(jax.random.fold_in(own_key, 6), axis_at), (blocks,), jnp.float32, low / len(cuts), largest / len(cuts))
        return jnp.repeat(jnp.exp(draws), extent[axis_at] // blocks).reshape((-1,) + (1,) * (len(extent) - axis_at - 1))

    level = one(*cuts[0])
    for cut in cuts[1:]:
        level = level * one(*cut)
    return level


def profile(number_of, total, limit, skew):
    weights = [(1 << 20) // math.isqrt(rank ** skew) + 1 for rank in range(2, number_of + 1)]
    rest, given = total - limit - (number_of - 1), [1] * (number_of - 1)
    while rest > 0:
        movable = [i for i in range(number_of - 1) if given[i] < limit]
        mass, budget = sum([weights[i] for i in movable]), rest
        for i in movable:
            more = min(limit - given[i], max(1, budget * weights[i] // mass), rest)
            given[i] = given[i] + more
            rest = rest - more
    return np.array([limit] + given)


def ragged(stream_key, amount, total, limit, skew):
    if amount == 2:
        one = jax.random.randint(stream_key, (), max(1, total - limit), min(limit, total - 1) + 1)
        return jnp.stack([one, total - one])
    tallies = jnp.asarray(profile(amount, total, limit, skew), jnp.int32)
    pairs = (amount - 1) // 2
    donor, sink = tallies[1:1 + 2 * pairs:2], tallies[2:2 + 2 * pairs:2]
    margin = jnp.minimum(donor - 1, limit - sink)
    passed = jax.random.randint(jax.random.fold_in(stream_key, 1), (pairs,), 0, 1 << 20) % (margin + 1)
    tallies = tallies.at[1:1 + 2 * pairs:2].set(donor - passed).at[2:2 + 2 * pairs:2].set(sink + passed)
    return tallies[jax.random.permutation(jax.random.fold_in(stream_key, 2), amount)]


def gaussian(key, dims, spread, limit, shards=(), held_as=jnp.bfloat16):
    entries = spread * jax.random.normal(key, dims, jnp.float32)
    if shards:
        entries = entries * block_levels(key, dims, shards, -0.22, 0.18)
    return jnp.clip(entries, -limit, limit).astype(held_as)


def heavy_noise(rng, dims, scale, most, pieces, heavy, kind=jnp.bfloat16):
    entries = scale * jax.random.normal(rng, dims, jnp.float32)
    if pieces:
        entries = entries * block_levels(rng, dims, pieces, -0.22, 0.18)
    return jnp.clip(with_spikes(entries, jax.random.fold_in(rng, 3), *heavy), -most, most).astype(kind)


def setup_inputs(seed: int = 0) -> dict:
    seeds = jax.random.split(jax.random.key(seed), 8)
    return {
        "hidden_in": heavy_noise(seeds[0], (FRAMES, D), 1.0, 6.0, ((0, 32),), (0, 1, 32, 2.75)),
        "rec_lengths": jax.vmap(lambda own: ragged(own, REC, FRAMES_G, MOST, 2))(jax.random.split(seeds[1], GROUPS)).reshape((GROUPS, REC)).astype(jnp.int32),
        "token_positions": draw_token_positions(jax.random.fold_in(seeds[7], 71), 0),
        "thinker_grad": gaussian(seeds[3], (THINK_ALL, D), 1.0, 6.0, ((0, 32),)),
        "norm_gain": jnp.clip(1.0 + 0.15 * jax.random.normal(seeds[4], (D,), jnp.float32), 0.25, 1.75),
        "norm_bias": gaussian(seeds[5], (D,), 0.5, 3.0, (), jnp.float32),
        "qkv_weight": draw_qkv_weight(jax.random.fold_in(seeds[7], 71), 0),
    }


norm_eps = 1e-05

def norm_forward(rows, gain, bias):
    rows_f32 = rows.astype(jnp.float32)
    mean_row = lax.optimization_barrier(jnp.mean(rows_f32, axis=-1, keepdims=True))
    centered = rows_f32 - mean_row
    variance = lax.optimization_barrier(jnp.mean(centered * centered, axis=-1, keepdims=True))
    inv_std = lax.rsqrt(variance + norm_eps)
    standard = centered * inv_std
    normalized = (standard * gain + bias).astype(jnp.bfloat16)
    return (normalized, standard, inv_std)

def norm_backward(norm_grad, standard, inv_std, gain):
    scaled = norm_grad * gain
    result = inv_std * (scaled - lax.optimization_barrier(jnp.mean(scaled, axis=-1, keepdims=True)) - standard * lax.optimization_barrier(jnp.mean(scaled * standard, axis=-1, keepdims=True)))
    return result.astype(jnp.bfloat16)

def segment_ids(lengths, count):
    ends = jnp.cumsum(lengths.astype(jnp.int32))
    frame_ids = jnp.arange(count, dtype=jnp.int32)
    return lax.optimization_barrier(jnp.sum((frame_ids[:, None] >= ends[None, :]).astype(jnp.int32), axis=1))

def head_backward(queries, keys_in, values, out_grad, segments, score_scale):
    scores = jnp.dot(queries, keys_in.T, preferred_element_type=jnp.float32)
    same_rec = segments[:, None] == segments[None, :]
    scores = jnp.where(same_rec, scores * score_scale, -1e+30)
    row_max = lax.optimization_barrier(jnp.max(scores, axis=-1, keepdims=True))
    expo = jnp.where(same_rec, jnp.exp(scores - row_max), 0.0)
    attn_weights = expo / lax.optimization_barrier(jnp.sum(expo, axis=-1, keepdims=True))
    weight_grads = jnp.dot(out_grad, values.T, preferred_element_type=jnp.float32)
    row_dot = lax.optimization_barrier(jnp.sum(attn_weights * weight_grads, axis=-1, keepdims=True))
    score_grad = (attn_weights * (weight_grads - row_dot)).astype(jnp.bfloat16)
    weights_low = attn_weights.astype(jnp.bfloat16)
    value_grad = jnp.dot(weights_low.T, out_grad, preferred_element_type=jnp.float32)
    query_grad = jnp.dot(score_grad, keys_in, preferred_element_type=jnp.float32) * score_scale
    key_grad = jnp.dot(score_grad.T, queries, preferred_element_type=jnp.float32) * score_scale
    return (query_grad, key_grad, value_grad)

def reference(hidden_in, rec_lengths, token_positions, thinker_grad, norm_gain, norm_bias, qkv_weight):
    groups = FRAMES // FRAMES_G
    score_scale = HD ** (-0.5)
    weight_flat = qkv_weight.reshape(D, 3 * D)
    frames_all = hidden_in.reshape(groups, FRAMES_G, D)
    positions_all = token_positions.reshape(groups, FRAMES_G)
    thinker_all = thinker_grad.reshape(groups, THINK_G, D)

    def group_step(total, items):
        rows, lengths, positions, thinker_rows = items
        normalized, standard, inv_std = norm_forward(rows, norm_gain, norm_bias)
        projected = jnp.dot(normalized, weight_flat, preferred_element_type=jnp.float32)
        projected = projected.astype(jnp.bfloat16).reshape(FRAMES_G, 3, HEADS, HD)
        out_grad = jnp.take(thinker_rows, positions, axis=0).reshape(FRAMES_G, HEADS, HD)
        segments = segment_ids(lengths, FRAMES_G)

        def one_head(head):
            return head_backward(projected[:, 0, head], projected[:, 1, head], projected[:, 2, head], out_grad[:, head], segments, score_scale)
        query_grad, key_grad, value_grad = lax.map(one_head, jnp.arange(HEADS, dtype=jnp.int32))
        stacked = jnp.stack([query_grad, key_grad, value_grad], axis=0)
        proj_grad = jnp.transpose(stacked, (2, 0, 1, 3)).astype(jnp.bfloat16).reshape(FRAMES_G, 3 * D)
        norm_grad = jnp.dot(proj_grad, weight_flat.T, preferred_element_type=jnp.float32)
        weight_part = jnp.dot(normalized.T, proj_grad, preferred_element_type=jnp.float32)
        result = norm_backward(norm_grad, standard, inv_std, norm_gain)
        return (total + weight_part, result)
    start_total = jnp.zeros((D, 3 * D), jnp.float32)
    weight_total, grads = lax.scan(group_step, start_total, (frames_all, rec_lengths, positions_all, thinker_all))
    return (grads.reshape(FRAMES, D).astype(jnp.bfloat16), weight_total.reshape(D, 3, D))
```

```python
import functools
import math

import jax
import jax.numpy as jnp
from jax import lax
from jax.experimental import pallas as pl
from jax.experimental.pallas import tpu as pltpu
from jax.sharding import PartitionSpec as P

HD = 64
MESH = pl.DeviceIdType.MESH
VMEM_LIMIT = 56 * 1024 * 1024

norm_eps = 1e-05
NEG = -1e30


def norm_forward(rows, gain, bias):
    rows_f32 = rows.astype(jnp.float32)
    mean_row = jnp.mean(rows_f32, axis=-1, keepdims=True)
    centered = rows_f32 - mean_row
    variance = jnp.mean(centered * centered, axis=-1, keepdims=True)
    inv_std = lax.rsqrt(variance + norm_eps)
    standard = centered * inv_std
    normalized = (standard * gain + bias).astype(jnp.bfloat16)
    return (normalized, standard, inv_std)


def norm_backward(norm_grad, standard, inv_std, gain):
    scaled = norm_grad * gain
    result = inv_std * (
        scaled
        - jnp.mean(scaled, axis=-1, keepdims=True)
        - standard * jnp.mean(scaled * standard, axis=-1, keepdims=True)
    )
    return result.astype(jnp.bfloat16)


def gather_kernel(
    dp, frames, w_ref, n_ref, t_ref, wg_ref, ng_ref, tg_ref,
    w_send, w_recv, n_send, n_recv, t_send, t_recv, own_sem,
):
    line = dp // 2
    pairs = frames // 2
    i = lax.axis_index("dp")
    f = lax.axis_index("frame")
    x, p = lax.rem(i, 2), lax.div(i, 2)
    c, u = lax.rem(f, 2), lax.div(f, 2)
    mate = p * 2 + (1 - x)
    right, left = i + 2, i - 2
    has_right, has_left = p < line - 1, p > 0

    barrier = pltpu.get_barrier_semaphore()
    pl.semaphore_signal(barrier, inc=1, device_id=(mate, f), device_id_type=MESH)

    @pl.when(has_right)
    def _():
        pl.semaphore_signal(barrier, inc=1, device_id=(right, f), device_id_type=MESH)

    @pl.when(has_left)
    def _():
        pl.semaphore_signal(barrier, inc=1, device_id=(left, f), device_id_type=MESH)

    for step in range(1, frames):
        other = lax.rem(f + step, frames)
        pl.semaphore_signal(barrier, inc=1, device_id=(i, other), device_id_type=MESH)
    ends = jnp.where(has_right, 1, 0) + jnp.where(has_left, 1, 0)
    pl.semaphore_wait(barrier, frames + ends)

    def w_copy(src, slot, way, target):
        return pltpu.make_async_remote_copy(
            src_ref=src, dst_ref=wg_ref.at[slot],
            send_sem=w_send.at[way, slot], recv_sem=w_recv.at[slot],
            device_id=(target, f), device_id_type=MESH,
        )

    def n_copy(src, slot, way, target):
        return pltpu.make_async_remote_copy(
            src_ref=src, dst_ref=ng_ref.at[slot],
            send_sem=n_send.at[way, slot], recv_sem=n_recv.at[slot],
            device_id=(i, target), device_id_type=MESH,
        )

    def t_copy(target):
        return pltpu.make_async_remote_copy(
            src_ref=t_ref.at[target], dst_ref=tg_ref.at[f],
            send_sem=t_send.at[target], recv_sem=t_recv.at[f],
            device_id=(i, target), device_id_type=MESH,
        )

    @pl.when(has_right)
    def _():
        w_copy(w_ref, i, 0, right).start()

    @pl.when(has_left)
    def _():
        w_copy(w_ref, i, 1, left).start()

    w_copy(w_ref, i, 2, mate).start()
    sibling = u * 2 + (1 - c)
    for step in range(1, pairs):
        far = lax.rem(u + step, pairs) * 2 + c
        n_copy(n_ref, f, step, far).start()
    n_copy(n_ref, f, 0, sibling).start()
    for step in range(1, frames):
        t_copy(lax.rem(f + step, frames)).start()
    own_w = pltpu.make_async_copy(w_ref, wg_ref.at[i], own_sem.at[0])
    own_n = pltpu.make_async_copy(n_ref, ng_ref.at[f], own_sem.at[1])
    own_t = pltpu.make_async_copy(t_ref.at[f], tg_ref.at[f], own_sem.at[2])
    own_w.start()
    own_n.start()
    own_t.start()

    def relay(step):
        from_left = i - 2 * step
        from_right = i + 2 * step

        @pl.when(p - step >= 0)
        def _():
            w_copy(w_ref, from_left, 0, mate).wait_recv()

            @pl.when(has_right)
            def _():
                w_copy(wg_ref.at[from_left], from_left, 0, right).start()

            w_copy(wg_ref.at[from_left], from_left, 2, mate).start()

        @pl.when(p + step <= line - 1)
        def _():
            w_copy(w_ref, from_right, 1, mate).wait_recv()

            @pl.when(has_left)
            def _():
                w_copy(wg_ref.at[from_right], from_right, 1, left).start()

            w_copy(wg_ref.at[from_right], from_right, 2, mate).start()

    def relay_norm():
        for step in range(1, pairs):
            far = lax.rem(u + step, pairs) * 2 + c
            n_copy(n_ref, far, 0, sibling).wait_recv()
            n_copy(ng_ref.at[far], far, 0, sibling).start()

    for step in range(1, min(line, 3)):
        relay(step)
    relay_norm()
    if line > 3:
        lax.fori_loop(3, line, lambda s, z: (relay(s), z)[1], 0)

    def finish(q, z):
        w_copy(w_ref, q * 2 + (1 - x), 2, mate).wait_recv()
        w_copy(w_ref, q * 2 + x, 2, mate).wait_send()

        @pl.when(jnp.logical_and(q <= p, has_right))
        def _():
            w_copy(w_ref, q * 2 + x, 0, right).wait_send()

        @pl.when(jnp.logical_and(q >= p, has_left))
        def _():
            w_copy(w_ref, q * 2 + x, 1, left).wait_send()

        return z

    for step in range(1, pairs):
        far = lax.rem(u + step, pairs) * 2 + c
        n_copy(n_ref, f, step, far).wait_send()
        n_copy(n_ref, far, 0, sibling).wait_send()
    n_copy(n_ref, f, 0, sibling).wait_send()
    for v in range(pairs):
        n_copy(n_ref, v * 2 + (1 - c), 0, sibling).wait_recv()
    for step in range(1, frames):
        other = lax.rem(f + step, frames)
        t_copy(other).wait_send()
        pltpu.make_async_remote_copy(
            src_ref=t_ref.at[other], dst_ref=tg_ref.at[other],
            send_sem=t_send.at[other], recv_sem=t_recv.at[other],
            device_id=(i, other), device_id_type=MESH,
        ).wait_recv()
    lax.fori_loop(0, line, finish, 0)
    own_w.wait()
    own_n.wait()
    own_t.wait()


def gather_all(dp, frames, weight, normalized, thinker):
    dma = pltpu.SemaphoreType.DMA
    any_spec = pl.BlockSpec(memory_space=pl.ANY)
    pairs = frames // 2
    moved = 2 * (dp * weight.size + frames * normalized.size + thinker.size)
    return pl.pallas_call(
        functools.partial(gather_kernel, dp, frames),
        out_shape=(
            jax.ShapeDtypeStruct((dp,) + weight.shape, weight.dtype),
            jax.ShapeDtypeStruct((frames,) + normalized.shape, normalized.dtype),
            jax.ShapeDtypeStruct(thinker.shape, thinker.dtype),
        ),
        in_specs=[any_spec] * 3,
        out_specs=(any_spec,) * 3,
        scratch_shapes=[
            dma((3, dp)), dma((dp,)),
            dma((pairs, frames)), dma((frames,)),
            dma((frames,)), dma((frames,)),
            dma((3,)),
        ],
        compiler_params=pltpu.CompilerParams(
            collective_id=0, has_side_effects=True, vmem_limit_bytes=VMEM_LIMIT
        ),
        cost_estimate=pl.CostEstimate(flops=0, bytes_accessed=2 * moved, transcendentals=0),
        name="gather_all",
    )(weight, normalized, thinker)


def local_kernel(
    rows_tile, tile_q, windows, len_ref, pos_ref, n_ref, w_ref, t_ref, ng_ref, wp_ref,
    q_s, k_s, v_s, g_s, kt_s, dq_s, dk_s, dv_s, dk_acc, dv_acc, grad_s,
):
    length, width = n_ref.shape
    cols = w_ref.shape[1]
    heads = cols // (3 * HD)
    recs = len_ref.shape[1]
    slack = t_ref.shape[0] - length
    scale = HD ** (-0.5)
    expo_scale = scale * math.log2(math.e)

    ends = []
    total = 0
    for r in range(recs):
        total = total + len_ref[0, r]
        ends.append(total)

    @pl.loop(0, length // rows_tile)
    def _(t):
        r0 = pl.multiple_of(t * rows_tile, rows_tile)
        rows = pl.ds(r0, rows_tile)
        proj = jnp.dot(n_ref[rows, :], w_ref[...], preferred_element_type=jnp.float32)
        proj = proj.astype(jnp.bfloat16)
        frame_ids = r0 + lax.broadcasted_iota(jnp.int32, (rows_tile, HD), 0)
        lane = lax.broadcasted_iota(jnp.int32, (rows_tile, HD), 1)
        seg = jnp.zeros((rows_tile, HD), jnp.int32)
        for end in ends:
            seg = seg + jnp.where(frame_ids >= end, 1, 0)
        same = seg == lane
        q_mask = jnp.where(jnp.logical_or(same, lane >= recs), 0.0, NEG).astype(jnp.bfloat16)
        k_mask = jnp.where(same, 1.0, 0.0).astype(jnp.bfloat16)
        cover = rows_tile + slack
        col = r0 + lax.broadcasted_iota(jnp.int32, (rows_tile, cover), 1)
        pick = jnp.where(col == pos_ref[rows, :], 1.0, 0.0).astype(jnp.bfloat16)
        out_grad = jnp.dot(
            pick, t_ref[pl.ds(r0, cover), :], preferred_element_type=jnp.float32
        ).astype(jnp.bfloat16)
        for h in range(heads):
            base = 3 * HD * h
            keys = proj[:, base + HD:base + 2 * HD]
            q_s[h, rows, 0:HD] = proj[:, base:base + HD]
            q_s[h, rows, HD:2 * HD] = q_mask
            k_s[h, rows, 0:HD] = keys
            k_s[h, rows, HD:2 * HD] = k_mask
            kt_s[h, :, rows] = keys.T
            v_s[h, rows, :] = proj[:, base + 2 * HD:base + 3 * HD]
            g_s[h, rows, :] = out_grad[:, h * HD:(h + 1) * HD]

    tiles = length // tile_q
    nt = (((1,), (1,)), ((), ()))

    @pl.loop(0, heads)
    def _(h):
        dk_acc[...] = jnp.zeros_like(dk_acc)
        dv_acc[...] = jnp.zeros_like(dv_acc)

        @pl.loop(0, tiles)
        def _(t):
            q0 = pl.multiple_of(t * tile_q, tile_q)
            q_last = q0 + tile_q - 1
            low = jnp.int32(0)
            high = jnp.int32(length)
            for end in ends:
                low = jnp.where(end <= q0, jnp.maximum(low, end), low)
                high = jnp.where(end > q_last, jnp.minimum(high, end), high)
            low = (low // 128) * 128
            need = high - low

            def attend(window):
                start = pl.multiple_of(jnp.minimum(low, length - window), 128)
                span = pl.ds(start, window)
                q_rows = q_s[h, pl.ds(q0, tile_q), :]
                g_rows = g_s[h, pl.ds(q0, tile_q), :]
                scores = lax.dot_general(
                    k_s[h, span, :], q_rows, nt, preferred_element_type=jnp.float32
                )
                grads = lax.dot_general(
                    v_s[h, span, :], g_rows, nt, preferred_element_type=jnp.float32
                )
                top = jnp.max(scores, axis=0, keepdims=True)
                expo = jnp.exp2((scores - top) * expo_scale)
                weights = expo * (1.0 / jnp.sum(expo, axis=0, keepdims=True))
                row_dot = jnp.sum(weights * grads, axis=0, keepdims=True)
                score_grad = (weights * (grads - row_dot)).astype(jnp.bfloat16)
                dv_acc[span, :] += jnp.dot(
                    weights.astype(jnp.bfloat16), g_rows, preferred_element_type=jnp.float32
                )
                dk_acc[span, :] += jnp.dot(
                    score_grad, q_rows[:, 0:HD], preferred_element_type=jnp.float32
                )
                dq_t = jnp.dot(kt_s[h, :, span], score_grad, preferred_element_type=jnp.float32)
                dq_s[h, pl.ds(q0, tile_q), :] = (dq_t * scale).T.astype(jnp.bfloat16)

            smaller = 0
            for window in windows:
                @pl.when(jnp.logical_and(need > smaller, need <= window))
                def _(window=window):
                    attend(window)
                smaller = window

        dk_s[h] = (dk_acc[...] * scale).astype(jnp.bfloat16)
        dv_s[h] = dv_acc[...].astype(jnp.bfloat16)

    @pl.loop(0, length // rows_tile)
    def _(t):
        rows = pl.ds(pl.multiple_of(t * rows_tile, rows_tile), rows_tile)
        parts = []
        for h in range(heads):
            parts += [dq_s[h, rows, :], dk_s[h, rows, :], dv_s[h, rows, :]]
        grad = jnp.concatenate(parts, axis=1)
        grad_s[rows, :] = grad
        ng_ref[rows, :] = lax.dot_general(
            grad, w_ref[...], nt, preferred_element_type=jnp.float32
        ).astype(jnp.bfloat16)

    @pl.loop(0, width // rows_tile)
    def _(t):
        rows = pl.ds(pl.multiple_of(t * rows_tile, rows_tile), rows_tile)
        wp_ref[rows, :] = lax.dot_general(
            n_ref[:, rows], grad_s[...], (((0,), (0,)), ((), ())),
            preferred_element_type=jnp.float32,
        ).astype(jnp.bfloat16)


def local_work(lengths, positions, group_norm, weight, thinker):
    length, width = group_norm.shape
    cols = weight.shape[1]
    heads = cols // (3 * HD)
    rows_tile = 256
    tile_q = 256
    windows = tuple(w for w in (512, 768) if w < length) + (length,)
    vmem = pl.BlockSpec(memory_space=pltpu.VMEM)
    bf16, f32 = jnp.bfloat16, jnp.float32
    return pl.pallas_call(
        functools.partial(local_kernel, rows_tile, tile_q, windows),
        out_shape=(
            jax.ShapeDtypeStruct((length, width), bf16),
            jax.ShapeDtypeStruct((width, cols), bf16),
        ),
        in_specs=[pl.BlockSpec(memory_space=pltpu.SMEM)] + [vmem] * 4,
        out_specs=(vmem, vmem),
        scratch_shapes=[
            pltpu.VMEM((heads, length, 2 * HD), bf16),
            pltpu.VMEM((heads, length, 2 * HD), bf16),
            pltpu.VMEM((heads, length, HD), bf16),
            pltpu.VMEM((heads, length, HD), bf16),
            pltpu.VMEM((heads, HD, length), bf16),
            pltpu.VMEM((heads, length, HD), bf16),
            pltpu.VMEM((heads, length, HD), bf16),
            pltpu.VMEM((heads, length, HD), bf16),
            pltpu.VMEM((length, HD), f32),
            pltpu.VMEM((length, HD), f32),
            pltpu.VMEM((length, cols), bf16),
        ],
        compiler_params=pltpu.CompilerParams(vmem_limit_bytes=VMEM_LIMIT),
        name="local_work",
    )(lengths, positions, group_norm, weight, thinker)


def per_device(
    hidden_in, rec_lengths, token_positions, thinker_grad, norm_gain, norm_bias, qkv_weight
):
    frame_count = lax.axis_size("frame")
    dp_count = lax.axis_size("dp")
    own_rows, three, head_cols = qkv_weight.shape
    heads = head_cols // HD
    width = hidden_in.shape[1]
    group_frames = token_positions.shape[0]
    think_rows = thinker_grad.shape[0]
    normalized, standard, inv_std = norm_forward(hidden_in, norm_gain, norm_bias)
    by_head = qkv_weight.reshape(own_rows, 3, heads, HD).transpose(0, 2, 1, 3)
    by_head = by_head.reshape(own_rows, 3 * head_cols)
    by_target = thinker_grad.reshape(think_rows, frame_count, head_cols).transpose(1, 0, 2)
    weight, group_norm, moved = gather_all(dp_count, frame_count, by_head, normalized, by_target)
    norm_part, weight_part = local_work(
        rec_lengths,
        token_positions.reshape(group_frames, 1),
        group_norm.reshape(group_frames, width),
        weight.reshape(width, 3 * head_cols),
        moved.reshape(frame_count * think_rows, head_cols),
    )
    norm_grad = lax.psum_scatter(
        norm_part, "frame", scatter_dimension=0, tiled=True
    ).astype(jnp.float32)
    weight_grad = lax.psum_scatter(
        weight_part, "dp", scatter_dimension=0, tiled=True
    ).astype(jnp.float32)
    weight_grad = weight_grad.reshape(own_rows, heads, 3, HD).transpose(0, 2, 1, 3)
    weight_grad = weight_grad.reshape(own_rows, 3, head_cols)
    hidden_grad = norm_backward(norm_grad, standard, inv_std, norm_gain)
    return (hidden_grad, weight_grad)


def solution(mesh):
    placed = (
        P(("dp", "frame"), None),
        P("dp", None),
        P("dp"),
        P(("dp", "frame"), None),
        P(),
        P(),
        P("dp", None, "frame"),
    )
    return jax.shard_map(
        per_device,
        mesh=mesh,
        in_specs=placed,
        out_specs=(P(("dp", "frame"), None), P("dp", None, "frame")),
        check_vma=False,
    )
```

```python
import functools
import math

import jax
import jax.numpy as jnp
from jax import lax
from jax.experimental import pallas as pl
from jax.experimental.pallas import tpu as pltpu
from jax.sharding import PartitionSpec as P

HD = 64
MESH = pl.DeviceIdType.MESH
VMEM_LIMIT = 56 * 1024 * 1024

norm_eps = 1e-05
NEG = -1e30


def norm_forward(rows, gain, bias):
    rows_f32 = rows.astype(jnp.float32)
    mean_row = jnp.mean(rows_f32, axis=-1, keepdims=True)
    centered = rows_f32 - mean_row
    variance = jnp.mean(centered * centered, axis=-1, keepdims=True)
    inv_std = lax.rsqrt(variance + norm_eps)
    standard = centered * inv_std
    normalized = (standard * gain + bias).astype(jnp.bfloat16)
    return (normalized, standard, inv_std)


def norm_backward(norm_grad, standard, inv_std, gain):
    scaled = norm_grad * gain
    result = inv_std * (
        scaled
        - jnp.mean(scaled, axis=-1, keepdims=True)
        - standard * jnp.mean(scaled * standard, axis=-1, keepdims=True)
    )
    return result.astype(jnp.bfloat16)


def gather_kernel(
    dp, frames, w_in, h_in, gain_ref, bias_ref, t_in, wg_ref, ng_ref, tg_ref,
    w_ref, n_ref, t_ref, w_send, w_recv, n_send, n_recv, t_send, t_recv, own_sem,
):
    head_cols = w_in.shape[2]
    line = dp // 2
    pairs = frames // 2
    i = lax.axis_index("dp")
    f = lax.axis_index("frame")
    x, p = lax.rem(i, 2), lax.div(i, 2)
    c, u = lax.rem(f, 2), lax.div(f, 2)
    mate = p * 2 + (1 - x)
    right, left = i + 2, i - 2
    has_right, has_left = p < line - 1, p > 0

    barrier = pltpu.get_barrier_semaphore()
    pl.semaphore_signal(barrier, inc=1, device_id=(mate, f), device_id_type=MESH)

    @pl.when(has_right)
    def _():
        pl.semaphore_signal(barrier, inc=1, device_id=(right, f), device_id_type=MESH)

    @pl.when(has_left)
    def _():
        pl.semaphore_signal(barrier, inc=1, device_id=(left, f), device_id_type=MESH)

    for step in range(1, frames):
        other = lax.rem(f + step, frames)
        pl.semaphore_signal(barrier, inc=1, device_id=(i, other), device_id_type=MESH)
    for h in range(head_cols // HD):
        for kind in range(3):
            at = (3 * h + kind) * HD
            w_ref[:, at:at + HD] = w_in[kind, :, h * HD:(h + 1) * HD]

    ends = jnp.where(has_right, 1, 0) + jnp.where(has_left, 1, 0)
    pl.semaphore_wait(barrier, frames + ends)

    def w_copy(src, slot, way, target):
        return pltpu.make_async_remote_copy(
            src_ref=src, dst_ref=wg_ref.at[slot],
            send_sem=w_send.at[way, slot], recv_sem=w_recv.at[slot],
            device_id=(target, f), device_id_type=MESH,
        )

    def n_copy(src, slot, way, target):
        return pltpu.make_async_remote_copy(
            src_ref=src, dst_ref=ng_ref.at[slot],
            send_sem=n_send.at[way, slot], recv_sem=n_recv.at[slot],
            device_id=(i, target), device_id_type=MESH,
        )

    def t_copy(target):
        return pltpu.make_async_remote_copy(
            src_ref=t_ref.at[target], dst_ref=tg_ref.at[f],
            send_sem=t_send.at[target], recv_sem=t_recv.at[f],
            device_id=(i, target), device_id_type=MESH,
        )

    @pl.when(has_right)
    def _():
        w_copy(w_ref, i, 0, right).start()

    @pl.when(has_left)
    def _():
        w_copy(w_ref, i, 1, left).start()

    w_copy(w_ref, i, 2, mate).start()
    sibling = u * 2 + (1 - c)
    n_ref[...] = norm_forward(h_in[...], gain_ref[...], bias_ref[...])[0]
    for step in range(1, pairs):
        far = lax.rem(u + step, pairs) * 2 + c
        n_copy(n_ref, f, step, far).start()
    n_copy(n_ref, f, 0, sibling).start()
    for target in range(frames):
        t_ref[target] = t_in[:, target * head_cols:(target + 1) * head_cols]
    for step in range(1, frames):
        t_copy(lax.rem(f + step, frames)).start()
    own_w = pltpu.make_async_copy(w_ref, wg_ref.at[i], own_sem.at[0])
    own_n = pltpu.make_async_copy(n_ref, ng_ref.at[f], own_sem.at[1])
    own_t = pltpu.make_async_copy(t_ref.at[f], tg_ref.at[f], own_sem.at[2])
    own_w.start()
    own_n.start()
    own_t.start()

    def relay(step):
        from_left = i - 2 * step
        from_right = i + 2 * step

        @pl.when(p - step >= 0)
        def _():
            w_copy(w_ref, from_left, 0, mate).wait_recv()

            @pl.when(has_right)
            def _():
                w_copy(wg_ref.at[from_left], from_left, 0, right).start()

            w_copy(wg_ref.at[from_left], from_left, 2, mate).start()

        @pl.when(p + step <= line - 1)
        def _():
            w_copy(w_ref, from_right, 1, mate).wait_recv()

            @pl.when(has_left)
            def _():
                w_copy(wg_ref.at[from_right], from_right, 1, left).start()

            w_copy(wg_ref.at[from_right], from_right, 2, mate).start()

    def relay_norm():
        for step in range(1, pairs):
            far = lax.rem(u + step, pairs) * 2 + c
            n_copy(n_ref, far, 0, sibling).wait_recv()
            n_copy(ng_ref.at[far], far, 0, sibling).start()

    for step in range(1, min(line, 3)):
        relay(step)
    relay_norm()
    if line > 3:
        lax.fori_loop(3, line, lambda s, z: (relay(s), z)[1], 0)

    def finish(q, z):
        w_copy(w_ref, q * 2 + (1 - x), 2, mate).wait_recv()
        w_copy(w_ref, q * 2 + x, 2, mate).wait_send()

        @pl.when(jnp.logical_and(q <= p, has_right))
        def _():
            w_copy(w_ref, q * 2 + x, 0, right).wait_send()

        @pl.when(jnp.logical_and(q >= p, has_left))
        def _():
            w_copy(w_ref, q * 2 + x, 1, left).wait_send()

        return z

    for step in range(1, pairs):
        far = lax.rem(u + step, pairs) * 2 + c
        n_copy(n_ref, f, step, far).wait_send()
        n_copy(n_ref, far, 0, sibling).wait_send()
    n_copy(n_ref, f, 0, sibling).wait_send()
    for v in range(pairs):
        n_copy(n_ref, v * 2 + (1 - c), 0, sibling).wait_recv()
    for step in range(1, frames):
        other = lax.rem(f + step, frames)
        t_copy(other).wait_send()
        pltpu.make_async_remote_copy(
            src_ref=t_ref.at[other], dst_ref=tg_ref.at[other],
            send_sem=t_send.at[other], recv_sem=t_recv.at[other],
            device_id=(i, other), device_id_type=MESH,
        ).wait_recv()
    lax.fori_loop(0, line, finish, 0)
    own_w.wait()
    own_n.wait()
    own_t.wait()


def gather_all(dp, frames, weight, hidden, gain, bias, thinker):
    dma = pltpu.SemaphoreType.DMA
    any_spec = pl.BlockSpec(memory_space=pl.ANY)
    vmem = pl.BlockSpec(memory_space=pltpu.VMEM)
    pairs = frames // 2
    kinds, own_rows, head_cols = weight.shape
    think_rows = thinker.shape[0]
    w_own = (own_rows, kinds * head_cols)
    t_own = (frames, think_rows, head_cols)
    moved = 2 * (dp * weight.size + frames * hidden.size + thinker.size)
    return pl.pallas_call(
        functools.partial(gather_kernel, dp, frames),
        out_shape=(
            jax.ShapeDtypeStruct((dp,) + w_own, weight.dtype),
            jax.ShapeDtypeStruct((frames,) + hidden.shape, hidden.dtype),
            jax.ShapeDtypeStruct(t_own, thinker.dtype),
        ),
        in_specs=[vmem] * 5,
        out_specs=(any_spec,) * 3,
        scratch_shapes=[
            pltpu.VMEM(w_own, weight.dtype),
            pltpu.VMEM(hidden.shape, hidden.dtype),
            pltpu.VMEM(t_own, thinker.dtype),
            dma((3, dp)), dma((dp,)),
            dma((pairs, frames)), dma((frames,)),
            dma((frames,)), dma((frames,)),
            dma((3,)),
        ],
        compiler_params=pltpu.CompilerParams(
            collective_id=0, has_side_effects=True, vmem_limit_bytes=VMEM_LIMIT
        ),
        cost_estimate=pl.CostEstimate(flops=0, bytes_accessed=2 * moved, transcendentals=0),
        name="gather_all",
    )(weight, hidden, gain, bias, thinker)


def local_kernel(
    rows_tile, tile_q, windows, len_ref, pos_ref, n_ref, w_ref, t_ref, ng_ref, wp_ref,
    q_s, k_s, v_s, g_s, kt_s, dq_s, dk_s, dv_s, dk_acc, dv_acc, grad_s,
):
    length, width = n_ref.shape
    cols = w_ref.shape[1]
    heads = cols // (3 * HD)
    recs = len_ref.shape[1]
    slack = t_ref.shape[0] - length
    scale = HD ** (-0.5)
    expo_scale = scale * math.log2(math.e)

    ends = []
    total = 0
    for r in range(recs):
        total = total + len_ref[0, r]
        ends.append(total)

    @pl.loop(0, length // rows_tile)
    def _(t):
        r0 = pl.multiple_of(t * rows_tile, rows_tile)
        rows = pl.ds(r0, rows_tile)
        proj = jnp.dot(n_ref[rows, :], w_ref[...], preferred_element_type=jnp.float32)
        proj = proj.astype(jnp.bfloat16)
        frame_ids = r0 + lax.broadcasted_iota(jnp.int32, (rows_tile, HD), 0)
        lane = lax.broadcasted_iota(jnp.int32, (rows_tile, HD), 1)
        seg = jnp.zeros((rows_tile, HD), jnp.int32)
        for end in ends:
            seg = seg + jnp.where(frame_ids >= end, 1, 0)
        same = seg == lane
        q_mask = jnp.where(jnp.logical_or(same, lane >= recs), 0.0, NEG).astype(jnp.bfloat16)
        k_mask = jnp.where(same, 1.0, 0.0).astype(jnp.bfloat16)
        cover = rows_tile + slack
        col = r0 + lax.broadcasted_iota(jnp.int32, (rows_tile, cover), 1)
        places = jnp.broadcast_to(pos_ref[:, rows], (128, rows_tile)).T[:, 0:1]
        pick = jnp.where(col == places, 1.0, 0.0).astype(jnp.bfloat16)
        out_grad = jnp.dot(
            pick, t_ref[pl.ds(r0, cover), :], preferred_element_type=jnp.float32
        ).astype(jnp.bfloat16)
        for h in range(heads):
            base = 3 * HD * h
            keys = proj[:, base + HD:base + 2 * HD]
            q_s[h, rows, 0:HD] = proj[:, base:base + HD]
            q_s[h, rows, HD:2 * HD] = q_mask
            k_s[h, rows, 0:HD] = keys
            k_s[h, rows, HD:2 * HD] = k_mask
            kt_s[h, :, rows] = keys.T
            v_s[h, rows, :] = proj[:, base + 2 * HD:base + 3 * HD]
            g_s[h, rows, :] = out_grad[:, h * HD:(h + 1) * HD]

    tiles = length // tile_q
    nt = (((1,), (1,)), ((), ()))

    @pl.loop(0, heads)
    def _(h):
        dk_acc[...] = jnp.zeros_like(dk_acc)
        dv_acc[...] = jnp.zeros_like(dv_acc)

        @pl.loop(0, tiles)
        def _(t):
            q0 = pl.multiple_of(t * tile_q, tile_q)
            q_last = q0 + tile_q - 1
            low = jnp.int32(0)
            high = jnp.int32(length)
            for end in ends:
                low = jnp.where(end <= q0, jnp.maximum(low, end), low)
                high = jnp.where(end > q_last, jnp.minimum(high, end), high)
            low = (low // 128) * 128
            need = high - low

            def attend(window):
                start = pl.multiple_of(jnp.minimum(low, length - window), 128)
                span = pl.ds(start, window)
                q_rows = q_s[h, pl.ds(q0, tile_q), :]
                g_rows = g_s[h, pl.ds(q0, tile_q), :]
                scores = lax.dot_general(
                    k_s[h, span, :], q_rows, nt, preferred_element_type=jnp.float32
                )
                grads = lax.dot_general(
                    v_s[h, span, :], g_rows, nt, preferred_element_type=jnp.float32
                )
                top = jnp.max(scores, axis=0, keepdims=True)
                expo = jnp.exp2((scores - top) * expo_scale)
                weights = expo * (1.0 / jnp.sum(expo, axis=0, keepdims=True))
                row_dot = jnp.sum(weights * grads, axis=0, keepdims=True)
                score_grad = (weights * (grads - row_dot)).astype(jnp.bfloat16)
                dv_acc[span, :] += jnp.dot(
                    weights.astype(jnp.bfloat16), g_rows, preferred_element_type=jnp.float32
                )
                dk_acc[span, :] += jnp.dot(
                    score_grad, q_rows[:, 0:HD], preferred_element_type=jnp.float32
                )
                dq_t = jnp.dot(kt_s[h, :, span], score_grad, preferred_element_type=jnp.float32)
                dq_s[h, pl.ds(q0, tile_q), :] = (dq_t * scale).T.astype(jnp.bfloat16)

            smaller = 0
            for window in windows:
                @pl.when(jnp.logical_and(need > smaller, need <= window))
                def _(window=window):
                    attend(window)
                smaller = window

        dk_s[h] = (dk_acc[...] * scale).astype(jnp.bfloat16)
        dv_s[h] = dv_acc[...].astype(jnp.bfloat16)

    @pl.loop(0, length // rows_tile)
    def _(t):
        rows = pl.ds(pl.multiple_of(t * rows_tile, rows_tile), rows_tile)
        parts = []
        for h in range(heads):
            parts += [dq_s[h, rows, :], dk_s[h, rows, :], dv_s[h, rows, :]]
        grad = jnp.concatenate(parts, axis=1)
        grad_s[rows, :] = grad
        ng_ref[rows, :] = lax.dot_general(
            grad, w_ref[...], nt, preferred_element_type=jnp.float32
        ).astype(jnp.bfloat16)

    @pl.loop(0, width // rows_tile)
    def _(t):
        rows = pl.ds(pl.multiple_of(t * rows_tile, rows_tile), rows_tile)
        wp_ref[rows, :] = lax.dot_general(
            n_ref[:, rows], grad_s[...], (((0,), (0,)), ((), ())),
            preferred_element_type=jnp.float32,
        ).astype(jnp.bfloat16)


def local_work(lengths, positions, group_norm, weight, thinker):
    length, width = group_norm.shape
    cols = weight.shape[1]
    heads = cols // (3 * HD)
    rows_tile = 256
    tile_q = 256
    windows = tuple(w for w in (512, 768) if w < length) + (length,)
    vmem = pl.BlockSpec(memory_space=pltpu.VMEM)
    bf16, f32 = jnp.bfloat16, jnp.float32
    return pl.pallas_call(
        functools.partial(local_kernel, rows_tile, tile_q, windows),
        out_shape=(
            jax.ShapeDtypeStruct((length, width), bf16),
            jax.ShapeDtypeStruct((width, cols), bf16),
        ),
        in_specs=[pl.BlockSpec(memory_space=pltpu.SMEM)] + [vmem] * 4,
        out_specs=(vmem, vmem),
        scratch_shapes=[
            pltpu.VMEM((heads, length, 2 * HD), bf16),
            pltpu.VMEM((heads, length, 2 * HD), bf16),
            pltpu.VMEM((heads, length, HD), bf16),
            pltpu.VMEM((heads, length, HD), bf16),
            pltpu.VMEM((heads, HD, length), bf16),
            pltpu.VMEM((heads, length, HD), bf16),
            pltpu.VMEM((heads, length, HD), bf16),
            pltpu.VMEM((heads, length, HD), bf16),
            pltpu.VMEM((length, HD), f32),
            pltpu.VMEM((length, HD), f32),
            pltpu.VMEM((length, cols), bf16),
        ],
        compiler_params=pltpu.CompilerParams(vmem_limit_bytes=VMEM_LIMIT),
        name="local_work",
    )(lengths, positions, group_norm, weight, thinker)


def reduce_kernel(
    dp, frames, wp_ref, np_ref, h_ref, gain_ref, wout_ref, hout_ref,
    from_mate, from_line, to_line, from_sib, from_far, to_far,
    m_send, m_recv, l_send, l_recv, s_send, s_recv, f_send, f_recv,
):
    line = dp // 2
    pairs = frames // 2
    i = lax.axis_index("dp")
    f = lax.axis_index("frame")
    x, p = lax.rem(i, 2), lax.div(i, 2)
    c, u = lax.rem(f, 2), lax.div(f, 2)
    mate = p * 2 + (1 - x)
    right, left = i + 2, i - 2
    has_right, has_left = p < line - 1, p > 0
    sibling = u * 2 + (1 - c)
    f32, bf16 = jnp.float32, jnp.bfloat16

    barrier = pltpu.get_barrier_semaphore()
    pl.semaphore_signal(barrier, inc=1, device_id=(mate, f), device_id_type=MESH)

    @pl.when(has_right)
    def _():
        pl.semaphore_signal(barrier, inc=1, device_id=(right, f), device_id_type=MESH)

    @pl.when(has_left)
    def _():
        pl.semaphore_signal(barrier, inc=1, device_id=(left, f), device_id_type=MESH)

    pl.semaphore_signal(barrier, inc=1, device_id=(i, sibling), device_id_type=MESH)
    for step in range(1, pairs):
        far = lax.rem(u + step, pairs) * 2 + c
        pl.semaphore_signal(barrier, inc=1, device_id=(i, far), device_id_type=MESH)
    ends = jnp.where(has_right, 1, 0) + jnp.where(has_left, 1, 0)
    pl.semaphore_wait(barrier, 1 + pairs + ends)

    def to_mate(q):
        return pltpu.make_async_remote_copy(
            src_ref=wp_ref.at[q * 2 + (1 - x)], dst_ref=from_mate.at[q],
            send_sem=m_send.at[q], recv_sem=m_recv.at[q],
            device_id=(mate, f), device_id_type=MESH,
        )

    def along(q, way, target):
        return pltpu.make_async_remote_copy(
            src_ref=to_line.at[q], dst_ref=from_line.at[way, q],
            send_sem=l_send.at[q], recv_sem=l_recv.at[way, q],
            device_id=(target, f), device_id_type=MESH,
        )

    def to_sibling(v):
        return pltpu.make_async_remote_copy(
            src_ref=np_ref.at[v * 2 + (1 - c)], dst_ref=from_sib.at[v],
            send_sem=s_send.at[v], recv_sem=s_recv.at[v],
            device_id=(i, sibling), device_id_type=MESH,
        )

    def to_other(v, slot):
        return pltpu.make_async_remote_copy(
            src_ref=to_far.at[v], dst_ref=from_far.at[slot],
            send_sem=f_send.at[v], recv_sem=f_recv.at[slot],
            device_id=(i, v * 2 + c), device_id_type=MESH,
        )

    ahead, behind = line - 1 - p, p

    def target_at(s):
        lower = jnp.where(s < ahead, line - 1 - s, s - ahead)
        upper = jnp.where(s < behind, s, line - 1 - (s - behind))
        return jnp.where(p < line // 2, lower, upper)

    for step in range(1, pairs):
        to_sibling(lax.rem(u + step, pairs)).start()
    lax.fori_loop(0, line, lambda s, z: (to_mate(target_at(s)).start(), z)[1], 0)
    to_sibling(u).start()

    for step in range(1, pairs):
        v = lax.rem(u + step, pairs)
        to_sibling(v).wait_recv()
        to_far[v] = (np_ref[v * 2 + c].astype(f32) + from_sib[v].astype(f32)).astype(bf16)
        to_other(v, u).start()

    def pass_on(s, z):
        q = target_at(s)
        to_mate(q).wait_recv()

        @pl.when(jnp.logical_and(q >= p, has_left))
        def _():
            along(q, 0, right).wait_recv()

        @pl.when(jnp.logical_and(q <= p, has_right))
        def _():
            along(q, 1, left).wait_recv()

        def own():
            return wp_ref[q * 2 + x].astype(f32) + from_mate[q].astype(f32)

        @pl.when(q > p)
        def _():
            @pl.when(has_left)
            def _():
                to_line[q] = (own() + from_line[0, q].astype(f32)).astype(bf16)

            @pl.when(jnp.logical_not(has_left))
            def _():
                to_line[q] = own().astype(bf16)

            along(q, 0, right).start()

        @pl.when(q < p)
        def _():
            @pl.when(has_right)
            def _():
                to_line[q] = (own() + from_line[1, q].astype(f32)).astype(bf16)

            @pl.when(jnp.logical_not(has_right))
            def _():
                to_line[q] = own().astype(bf16)

            along(q, 1, left).start()

        return z

    lax.fori_loop(0, line - 1, pass_on, 0)

    to_sibling(u).wait_recv()
    total = np_ref[f].astype(f32) + from_sib[u].astype(f32)
    for step in range(1, pairs):
        v = lax.rem(u + step, pairs)
        to_other(v, v).wait_recv()
        total = total + from_far[v].astype(f32)
    rows = h_ref[...].astype(f32)
    mean_row = jnp.mean(rows, axis=-1, keepdims=True)
    centered = rows - mean_row
    inv_std = lax.rsqrt(jnp.mean(centered * centered, axis=-1, keepdims=True) + norm_eps)
    hout_ref[...] = norm_backward(total, centered * inv_std, inv_std, gain_ref[...])

    pass_on(line - 1, 0)
    kinds, _, head_cols = wout_ref.shape
    zero = jnp.zeros(wp_ref.shape[1:], f32)

    @pl.when(jnp.logical_not(has_left))
    def _():
        from_line[0, p] = zero.astype(bf16)

    @pl.when(jnp.logical_not(has_right))
    def _():
        from_line[1, p] = zero.astype(bf16)

    final = wp_ref[i].astype(f32) + from_mate[p].astype(f32)
    final = final + from_line[0, p].astype(f32) + from_line[1, p].astype(f32)
    for h in range(head_cols // HD):
        for kind in range(kinds):
            at = (kinds * h + kind) * HD
            wout_ref[kind, :, h * HD:(h + 1) * HD] = final[:, at:at + HD]

    def sent(q, z):
        to_mate(q).wait_send()

        @pl.when(q != p)
        def _():
            along(q, 0, right).wait_send()

        return z

    lax.fori_loop(0, line, sent, 0)
    for v in range(pairs):
        to_sibling(v).wait_send()
    for step in range(1, pairs):
        v = lax.rem(u + step, pairs)
        to_other(v, u).wait_send()


def reduce_all(dp, frames, weight_part, norm_part, hidden, gain, heads):
    dma = pltpu.SemaphoreType.DMA
    vmem = pl.BlockSpec(memory_space=pltpu.VMEM)
    pairs, line = frames // 2, dp // 2
    bf16, f32 = jnp.bfloat16, jnp.float32
    own_rows, cols = weight_part.shape[1:]
    moved = 2 * (weight_part.size + norm_part.size)
    return pl.pallas_call(
        functools.partial(reduce_kernel, dp, frames),
        out_shape=(
            jax.ShapeDtypeStruct((3, own_rows, cols // 3), f32),
            jax.ShapeDtypeStruct(hidden.shape, bf16),
        ),
        in_specs=[vmem] * 4,
        out_specs=(vmem,) * 2,
        scratch_shapes=[
            pltpu.VMEM((line, own_rows, cols), bf16),
            pltpu.VMEM((2, line, own_rows, cols), bf16),
            pltpu.VMEM((line, own_rows, cols), bf16),
            pltpu.VMEM((pairs,) + hidden.shape, bf16),
            pltpu.VMEM((pairs,) + hidden.shape, bf16),
            pltpu.VMEM((pairs,) + hidden.shape, bf16),
            dma((line,)), dma((line,)), dma((line,)), dma((2, line)),
            dma((pairs,)), dma((pairs,)), dma((pairs,)), dma((pairs,)),
        ],
        compiler_params=pltpu.CompilerParams(
            collective_id=1, has_side_effects=True, vmem_limit_bytes=VMEM_LIMIT
        ),
        cost_estimate=pl.CostEstimate(flops=0, bytes_accessed=2 * moved, transcendentals=0),
        name="reduce_all",
    )(weight_part, norm_part, hidden, gain)


def per_device(
    hidden_in, rec_lengths, token_positions, thinker_grad, norm_gain, norm_bias, qkv_weight
):
    frame_count = lax.axis_size("frame")
    dp_count = lax.axis_size("dp")
    own_rows, three, head_cols = qkv_weight.shape
    heads = head_cols // HD
    own_frames, width = hidden_in.shape
    group_frames = token_positions.shape[0]
    think_rows = thinker_grad.shape[0]
    gain = norm_gain.reshape(1, width)
    weight, group_norm, moved = gather_all(
        dp_count, frame_count, qkv_weight.transpose(1, 0, 2), hidden_in,
        gain, norm_bias.reshape(1, width), thinker_grad,
    )
    norm_part, weight_part = local_work(
        rec_lengths,
        token_positions.reshape(1, group_frames),
        group_norm.reshape(group_frames, width),
        weight.reshape(width, 3 * head_cols),
        moved.reshape(frame_count * think_rows, head_cols),
    )
    weight_grad, hidden_grad = reduce_all(
        dp_count, frame_count,
        weight_part.reshape(dp_count, own_rows, 3 * head_cols),
        norm_part.reshape(frame_count, own_frames, width),
        hidden_in, gain, heads,
    )
    return (hidden_grad, weight_grad.transpose(1, 0, 2))


def solution(mesh):
    placed = (
        P(("dp", "frame"), None),
        P("dp", None),
        P("dp"),
        P(("dp", "frame"), None),
        P(),
        P(),
        P("dp", None, "frame"),
    )
    return jax.shard_map(
        per_device,
        mesh=mesh,
        in_specs=placed,
        out_specs=(P(("dp", "frame"), None), P("dp", None, "frame")),
        check_vma=False,
    )
```

```python
import functools
import math

import jax
import jax.numpy as jnp
from jax import lax
from jax.experimental import pallas as pl
from jax.experimental.pallas import tpu as pltpu
from jax.sharding import PartitionSpec as P

HD = 64
MESH = pl.DeviceIdType.MESH
VMEM_LIMIT = 56 * 1024 * 1024

norm_eps = 1e-05
NEG = -1e30


def norm_forward(rows, gain, bias):
    rows_f32 = rows.astype(jnp.float32)
    mean_row = jnp.mean(rows_f32, axis=-1, keepdims=True)
    centered = rows_f32 - mean_row
    variance = jnp.mean(centered * centered, axis=-1, keepdims=True)
    inv_std = lax.rsqrt(variance + norm_eps)
    standard = centered * inv_std
    normalized = (standard * gain + bias).astype(jnp.bfloat16)
    return (normalized, standard, inv_std)


def norm_backward(norm_grad, standard, inv_std, gain):
    scaled = norm_grad * gain
    result = inv_std * (
        scaled
        - jnp.mean(scaled, axis=-1, keepdims=True)
        - standard * jnp.mean(scaled * standard, axis=-1, keepdims=True)
    )
    return result.astype(jnp.bfloat16)


def part_kernel(w_ref, *out_refs):
    first = 0
    for out_ref in out_refs:
        heads = out_ref.shape[1] // (3 * HD)
        for h in range(heads):
            for kind in range(3):
                at = (3 * h + kind) * HD
                source = (first + h) * HD
                out_ref[:, at:at + HD] = w_ref[kind, :, source:source + HD]
        first += heads


def part_weight(weight, parts):
    vmem = pl.BlockSpec(memory_space=pltpu.VMEM)
    rows = weight.shape[1]
    return pl.pallas_call(
        part_kernel,
        out_shape=tuple(
            jax.ShapeDtypeStruct((rows, 3 * HD * heads), weight.dtype) for heads in parts
        ),
        in_specs=[vmem],
        out_specs=(vmem,) * len(parts),
        name="part_weight",
    )(weight)


def finish_kernel(wa_ref, wb_ref, h_ref, w_out, h_out):
    first = 0
    for ref in (wa_ref, wb_ref):
        heads = ref.shape[1] // (3 * HD)
        for h in range(heads):
            for kind in range(3):
                at = (3 * h + kind) * HD
                target = (first + h) * HD
                w_out[kind, :, target:target + HD] = ref[:, at:at + HD].astype(jnp.float32)
        first += heads
    h_out[...] = h_ref[...]


def finish(first_grad, second_grad, hidden_grad):
    vmem = pl.BlockSpec(memory_space=pltpu.VMEM)
    rows = first_grad.shape[0]
    cols = (first_grad.shape[1] + second_grad.shape[1]) // 3
    return pl.pallas_call(
        finish_kernel,
        out_shape=(
            jax.ShapeDtypeStruct((3, rows, cols), jnp.float32),
            jax.ShapeDtypeStruct(hidden_grad.shape, hidden_grad.dtype),
        ),
        in_specs=[vmem] * 3,
        out_specs=(vmem,) * 2,
        name="finish",
    )(first_grad, second_grad, hidden_grad)


def gather_kernel(
    dp, frames, w_ref, h_in, gain_ref, bias_ref, t_in, wg_ref, ng_ref, tg_ref,
    n_ref, t_ref, w_send, w_recv, n_send, n_recv, t_send, t_recv, own_sem,
):
    head_cols = t_in.shape[1] // frames
    line = dp // 2
    pairs = frames // 2
    i = lax.axis_index("dp")
    f = lax.axis_index("frame")
    x, p = lax.rem(i, 2), lax.div(i, 2)
    c, u = lax.rem(f, 2), lax.div(f, 2)
    mate = p * 2 + (1 - x)
    right, left = i + 2, i - 2
    has_right, has_left = p < line - 1, p > 0

    barrier = pltpu.get_barrier_semaphore()
    pl.semaphore_signal(barrier, inc=1, device_id=(mate, f), device_id_type=MESH)

    @pl.when(has_right)
    def _():
        pl.semaphore_signal(barrier, inc=1, device_id=(right, f), device_id_type=MESH)

    @pl.when(has_left)
    def _():
        pl.semaphore_signal(barrier, inc=1, device_id=(left, f), device_id_type=MESH)

    for step in range(1, frames):
        other = lax.rem(f + step, frames)
        pl.semaphore_signal(barrier, inc=1, device_id=(i, other), device_id_type=MESH)
    ends = jnp.where(has_right, 1, 0) + jnp.where(has_left, 1, 0)
    pl.semaphore_wait(barrier, frames + ends)

    def w_copy(src, slot, way, target):
        return pltpu.make_async_remote_copy(
            src_ref=src, dst_ref=wg_ref.at[slot],
            send_sem=w_send.at[way, slot], recv_sem=w_recv.at[slot],
            device_id=(target, f), device_id_type=MESH,
        )

    def n_copy(src, slot, way, target):
        return pltpu.make_async_remote_copy(
            src_ref=src, dst_ref=ng_ref.at[slot],
            send_sem=n_send.at[way, slot], recv_sem=n_recv.at[slot],
            device_id=(i, target), device_id_type=MESH,
        )

    def t_copy(target):
        return pltpu.make_async_remote_copy(
            src_ref=t_ref.at[target], dst_ref=tg_ref.at[f],
            send_sem=t_send.at[target], recv_sem=t_recv.at[f],
            device_id=(i, target), device_id_type=MESH,
        )

    @pl.when(has_right)
    def _():
        w_copy(w_ref, i, 0, right).start()

    @pl.when(has_left)
    def _():
        w_copy(w_ref, i, 1, left).start()

    w_copy(w_ref, i, 2, mate).start()
    sibling = u * 2 + (1 - c)
    n_ref[...] = norm_forward(
        h_in[...], gain_ref[...].reshape(1, -1), bias_ref[...].reshape(1, -1)
    )[0]
    for step in range(1, pairs):
        far = lax.rem(u + step, pairs) * 2 + c
        n_copy(n_ref, f, step, far).start()
    n_copy(n_ref, f, 0, sibling).start()
    for target in range(frames):
        t_ref[target] = t_in[:, target * head_cols:(target + 1) * head_cols]
    for step in range(1, frames):
        t_copy(lax.rem(f + step, frames)).start()
    own_w = pltpu.make_async_copy(w_ref, wg_ref.at[i], own_sem.at[0])
    own_n = pltpu.make_async_copy(n_ref, ng_ref.at[f], own_sem.at[1])
    own_t = pltpu.make_async_copy(t_ref.at[f], tg_ref.at[f], own_sem.at[2])
    own_w.start()
    own_n.start()
    own_t.start()

    def relay(step):
        from_left = i - 2 * step
        from_right = i + 2 * step

        @pl.when(p - step >= 0)
        def _():
            w_copy(w_ref, from_left, 0, mate).wait_recv()

            @pl.when(has_right)
            def _():
                w_copy(wg_ref.at[from_left], from_left, 0, right).start()

            w_copy(wg_ref.at[from_left], from_left, 2, mate).start()

        @pl.when(p + step <= line - 1)
        def _():
            w_copy(w_ref, from_right, 1, mate).wait_recv()

            @pl.when(has_left)
            def _():
                w_copy(wg_ref.at[from_right], from_right, 1, left).start()

            w_copy(wg_ref.at[from_right], from_right, 2, mate).start()

    def relay_norm():
        for step in range(1, pairs):
            far = lax.rem(u + step, pairs) * 2 + c
            n_copy(n_ref, far, 0, sibling).wait_recv()
            n_copy(ng_ref.at[far], far, 0, sibling).start()

    for step in range(1, min(line, 3)):
        relay(step)
    relay_norm()
    if line > 3:
        lax.fori_loop(3, line, lambda s, z: (relay(s), z)[1], 0)

    def finish(q, z):
        w_copy(w_ref, q * 2 + (1 - x), 2, mate).wait_recv()
        w_copy(w_ref, q * 2 + x, 2, mate).wait_send()

        @pl.when(jnp.logical_and(q <= p, has_right))
        def _():
            w_copy(w_ref, q * 2 + x, 0, right).wait_send()

        @pl.when(jnp.logical_and(q >= p, has_left))
        def _():
            w_copy(w_ref, q * 2 + x, 1, left).wait_send()

        return z

    for step in range(1, pairs):
        far = lax.rem(u + step, pairs) * 2 + c
        n_copy(n_ref, f, step, far).wait_send()
        n_copy(n_ref, far, 0, sibling).wait_send()
    n_copy(n_ref, f, 0, sibling).wait_send()
    for v in range(pairs):
        n_copy(n_ref, v * 2 + (1 - c), 0, sibling).wait_recv()
    for step in range(1, frames):
        other = lax.rem(f + step, frames)
        t_copy(other).wait_send()
        pltpu.make_async_remote_copy(
            src_ref=t_ref.at[other], dst_ref=tg_ref.at[other],
            send_sem=t_send.at[other], recv_sem=t_recv.at[other],
            device_id=(i, other), device_id_type=MESH,
        ).wait_recv()
    lax.fori_loop(0, line, finish, 0)
    own_w.wait()
    own_n.wait()
    own_t.wait()


def gather_all(dp, frames, weight, hidden, gain, bias, thinker):
    dma = pltpu.SemaphoreType.DMA
    any_spec = pl.BlockSpec(memory_space=pl.ANY)
    vmem = pl.BlockSpec(memory_space=pltpu.VMEM)
    pairs = frames // 2
    think_rows = thinker.shape[0]
    w_own = weight.shape
    t_own = (frames, think_rows, thinker.shape[1] // frames)
    moved = 2 * (dp * weight.size + frames * hidden.size + thinker.size)
    return pl.pallas_call(
        functools.partial(gather_kernel, dp, frames),
        out_shape=(
            jax.ShapeDtypeStruct((dp,) + w_own, weight.dtype),
            jax.ShapeDtypeStruct((frames,) + hidden.shape, hidden.dtype),
            jax.ShapeDtypeStruct(t_own, thinker.dtype),
        ),
        in_specs=[vmem] * 5,
        out_specs=(any_spec,) * 3,
        scratch_shapes=[
            pltpu.VMEM(hidden.shape, hidden.dtype),
            pltpu.VMEM(t_own, thinker.dtype),
            dma((3, dp)), dma((dp,)),
            dma((pairs, frames)), dma((frames,)),
            dma((frames,)), dma((frames,)),
            dma((3,)),
        ],
        compiler_params=pltpu.CompilerParams(
            collective_id=0, has_side_effects=True, vmem_limit_bytes=VMEM_LIMIT
        ),
        cost_estimate=pl.CostEstimate(flops=0, bytes_accessed=10 * moved, transcendentals=0),
        name="gather_all",
    )(weight, hidden, gain, bias, thinker)


def local_kernel(rows_tile, tile_q, windows, is_first, len_ref, n_ref, w_ref, *refs):
    if is_first:
        pos_ref, t_ref, og_ref, grad_s, wp_ref = refs[:5]
    else:
        og_ref, grad_a, w_a, ng_ref, wp_ref = refs[:5]
        grad_s = refs[-1]
    q_s, k_s, v_s, g_s, kt_s, dq_s, dk_s, dv_s, dk_acc, dv_acc = refs[5:15]
    length, width = n_ref.shape
    cols = w_ref.shape[1]
    heads = cols // (3 * HD)
    head_from = 0 if is_first else og_ref.shape[1] // HD - heads
    recs = len_ref.shape[1]
    scale = HD ** (-0.5)
    expo_scale = scale * math.log2(math.e)

    ends = []
    total = 0
    for r in range(recs):
        total = total + len_ref[0, r]
        ends.append(total)

    @pl.loop(0, length // rows_tile)
    def _(t):
        r0 = pl.multiple_of(t * rows_tile, rows_tile)
        rows = pl.ds(r0, rows_tile)
        proj = jnp.dot(n_ref[rows, :], w_ref[...], preferred_element_type=jnp.float32)
        proj = proj.astype(jnp.bfloat16)
        frame_ids = r0 + lax.broadcasted_iota(jnp.int32, (rows_tile, HD), 0)
        lane = lax.broadcasted_iota(jnp.int32, (rows_tile, HD), 1)
        seg = jnp.zeros((rows_tile, HD), jnp.int32)
        for end in ends:
            seg = seg + jnp.where(frame_ids >= end, 1, 0)
        same = seg == lane
        q_mask = jnp.where(jnp.logical_or(same, lane >= recs), 0.0, NEG).astype(jnp.bfloat16)
        k_mask = jnp.where(same, 1.0, 0.0).astype(jnp.bfloat16)
        if is_first:
            cover = rows_tile + t_ref.shape[0] - length
            col = r0 + lax.broadcasted_iota(jnp.int32, (rows_tile, cover), 1)
            places = jnp.broadcast_to(pos_ref[:, rows], (128, rows_tile)).T[:, 0:1]
            pick = jnp.where(col == places, 1.0, 0.0).astype(jnp.bfloat16)
            out_grad = jnp.dot(
                pick, t_ref[pl.ds(r0, cover), :], preferred_element_type=jnp.float32
            ).astype(jnp.bfloat16)
            og_ref[rows, :] = out_grad
        else:
            out_grad = og_ref[rows, :]
        for h in range(heads):
            base = 3 * HD * h
            keys = proj[:, base + HD:base + 2 * HD]
            q_s[h, rows, 0:HD] = proj[:, base:base + HD]
            q_s[h, rows, HD:2 * HD] = q_mask
            k_s[h, rows, 0:HD] = keys
            k_s[h, rows, HD:2 * HD] = k_mask
            kt_s[h, :, rows] = keys.T
            v_s[h, rows, :] = proj[:, base + 2 * HD:base + 3 * HD]
            at = (head_from + h) * HD
            g_s[h, rows, :] = out_grad[:, at:at + HD]

    tiles = length // tile_q
    nt = (((1,), (1,)), ((), ()))

    @pl.loop(0, heads)
    def _(h):
        dk_acc[...] = jnp.zeros_like(dk_acc)
        dv_acc[...] = jnp.zeros_like(dv_acc)

        @pl.loop(0, tiles)
        def _(t):
            q0 = pl.multiple_of(t * tile_q, tile_q)
            q_last = q0 + tile_q - 1
            low = jnp.int32(0)
            high = jnp.int32(length)
            for end in ends:
                low = jnp.where(end <= q0, jnp.maximum(low, end), low)
                high = jnp.where(end > q_last, jnp.minimum(high, end), high)
            low = (low // 128) * 128
            need = high - low

            def attend(window):
                start = pl.multiple_of(jnp.minimum(low, length - window), 128)
                span = pl.ds(start, window)
                q_rows = q_s[h, pl.ds(q0, tile_q), :]
                g_rows = g_s[h, pl.ds(q0, tile_q), :]
                scores = lax.dot_general(
                    k_s[h, span, :], q_rows, nt, preferred_element_type=jnp.float32
                )
                grads = lax.dot_general(
                    v_s[h, span, :], g_rows, nt, preferred_element_type=jnp.float32
                )
                top = jnp.max(scores, axis=0, keepdims=True)
                expo = jnp.exp2((scores - top) * expo_scale)
                weights = expo * (1.0 / jnp.sum(expo, axis=0, keepdims=True))
                row_dot = jnp.sum(weights * grads, axis=0, keepdims=True)
                score_grad = (weights * (grads - row_dot)).astype(jnp.bfloat16)
                dv_acc[span, :] += jnp.dot(
                    weights.astype(jnp.bfloat16), g_rows, preferred_element_type=jnp.float32
                )
                dk_acc[span, :] += jnp.dot(
                    score_grad, q_rows[:, 0:HD], preferred_element_type=jnp.float32
                )
                dq_t = jnp.dot(kt_s[h, :, span], score_grad, preferred_element_type=jnp.float32)
                dq_s[h, pl.ds(q0, tile_q), :] = (dq_t * scale).T.astype(jnp.bfloat16)

            smaller = 0
            for window in windows:
                @pl.when(jnp.logical_and(need > smaller, need <= window))
                def _(window=window):
                    attend(window)
                smaller = window

        dk_s[h] = (dk_acc[...] * scale).astype(jnp.bfloat16)
        dv_s[h] = dv_acc[...].astype(jnp.bfloat16)

    @pl.loop(0, length // rows_tile)
    def _(t):
        rows = pl.ds(pl.multiple_of(t * rows_tile, rows_tile), rows_tile)
        parts = []
        for h in range(heads):
            parts += [dq_s[h, rows, :], dk_s[h, rows, :], dv_s[h, rows, :]]
        grad = jnp.concatenate(parts, axis=1)
        grad_s[rows, :] = grad
        if not is_first:
            summed = lax.dot_general(grad, w_ref[...], nt, preferred_element_type=jnp.float32)
            summed = summed + lax.dot_general(
                grad_a[rows, :], w_a[...], nt, preferred_element_type=jnp.float32
            )
            ng_ref[rows, :] = summed.astype(jnp.bfloat16)

    @pl.loop(0, width // rows_tile)
    def _(t):
        rows = pl.ds(pl.multiple_of(t * rows_tile, rows_tile), rows_tile)
        wp_ref[rows, :] = lax.dot_general(
            n_ref[:, rows], grad_s[...], (((0,), (0,)), ((), ())),
            preferred_element_type=jnp.float32,
        ).astype(jnp.bfloat16)


def local_work(is_first, lengths, group_norm, weight, *rest):
    length, width = group_norm.shape
    cols = weight.shape[1]
    heads = cols // (3 * HD)
    rows_tile = 256
    tile_q = 256
    windows = tuple(w for w in (512, 768) if w < length) + (length,)
    vmem = pl.BlockSpec(memory_space=pltpu.VMEM)
    bf16, f32 = jnp.bfloat16, jnp.float32
    grad_type = (length, cols)
    if is_first:
        outs = ((length, rest[1].shape[1]), grad_type, (width, cols))
    else:
        outs = ((length, width), (width, cols))
    scratch = [
        pltpu.VMEM((heads, length, 2 * HD), bf16),
        pltpu.VMEM((heads, length, 2 * HD), bf16),
        pltpu.VMEM((heads, length, HD), bf16),
        pltpu.VMEM((heads, length, HD), bf16),
        pltpu.VMEM((heads, HD, length), bf16),
        pltpu.VMEM((heads, length, HD), bf16),
        pltpu.VMEM((heads, length, HD), bf16),
        pltpu.VMEM((heads, length, HD), bf16),
        pltpu.VMEM((length, HD), f32),
        pltpu.VMEM((length, HD), f32),
    ]
    if not is_first:
        scratch.append(pltpu.VMEM(grad_type, bf16))
    return pl.pallas_call(
        functools.partial(local_kernel, rows_tile, tile_q, windows, is_first),
        out_shape=tuple(jax.ShapeDtypeStruct(shape, bf16) for shape in outs),
        in_specs=[pl.BlockSpec(memory_space=pltpu.SMEM)] + [vmem] * (2 + len(rest)),
        out_specs=(vmem,) * len(outs),
        scratch_shapes=scratch,
        compiler_params=pltpu.CompilerParams(vmem_limit_bytes=VMEM_LIMIT),
        cost_estimate=pl.CostEstimate(
            flops=40 * heads * length * length * HD, bytes_accessed=4 * length * width,
            transcendentals=heads * length * length,
        ),
        name="local_first" if is_first else "local_second",
    )(lengths, group_norm, weight, *rest)


def reduce_kernel(
    dp, frames, wp_ref, np_ref, h_ref, gain_ref, wout_ref, hout_ref,
    from_mate, from_line, to_line, from_sib, from_far, to_far,
    m_send, m_recv, l_send, l_recv, s_send, s_recv, f_send, f_recv,
):
    line = dp // 2
    pairs = frames // 2
    i = lax.axis_index("dp")
    f = lax.axis_index("frame")
    x, p = lax.rem(i, 2), lax.div(i, 2)
    c, u = lax.rem(f, 2), lax.div(f, 2)
    mate = p * 2 + (1 - x)
    right, left = i + 2, i - 2
    has_right, has_left = p < line - 1, p > 0
    sibling = u * 2 + (1 - c)
    f32, bf16 = jnp.float32, jnp.bfloat16

    barrier = pltpu.get_barrier_semaphore()
    pl.semaphore_signal(barrier, inc=1, device_id=(mate, f), device_id_type=MESH)

    @pl.when(has_right)
    def _():
        pl.semaphore_signal(barrier, inc=1, device_id=(right, f), device_id_type=MESH)

    @pl.when(has_left)
    def _():
        pl.semaphore_signal(barrier, inc=1, device_id=(left, f), device_id_type=MESH)

    pl.semaphore_signal(barrier, inc=1, device_id=(i, sibling), device_id_type=MESH)
    for step in range(1, pairs):
        far = lax.rem(u + step, pairs) * 2 + c
        pl.semaphore_signal(barrier, inc=1, device_id=(i, far), device_id_type=MESH)
    ends = jnp.where(has_right, 1, 0) + jnp.where(has_left, 1, 0)
    pl.semaphore_wait(barrier, 1 + pairs + ends)

    def to_mate(q):
        return pltpu.make_async_remote_copy(
            src_ref=wp_ref.at[q * 2 + (1 - x)], dst_ref=from_mate.at[q],
            send_sem=m_send.at[q], recv_sem=m_recv.at[q],
            device_id=(mate, f), device_id_type=MESH,
        )

    def along(q, way, target):
        return pltpu.make_async_remote_copy(
            src_ref=to_line.at[q], dst_ref=from_line.at[way, q],
            send_sem=l_send.at[q], recv_sem=l_recv.at[way, q],
            device_id=(target, f), device_id_type=MESH,
        )

    def to_sibling(v):
        return pltpu.make_async_remote_copy(
            src_ref=np_ref.at[v * 2 + (1 - c)], dst_ref=from_sib.at[v],
            send_sem=s_send.at[v], recv_sem=s_recv.at[v],
            device_id=(i, sibling), device_id_type=MESH,
        )

    def to_other(v, slot):
        return pltpu.make_async_remote_copy(
            src_ref=to_far.at[v], dst_ref=from_far.at[slot],
            send_sem=f_send.at[v], recv_sem=f_recv.at[slot],
            device_id=(i, v * 2 + c), device_id_type=MESH,
        )

    ahead, behind = line - 1 - p, p

    def target_at(s):
        lower = jnp.where(s < ahead, line - 1 - s, s - ahead)
        upper = jnp.where(s < behind, s, line - 1 - (s - behind))
        return jnp.where(p < line // 2, lower, upper)

    for step in range(1, pairs):
        to_sibling(lax.rem(u + step, pairs)).start()
    lax.fori_loop(0, line, lambda s, z: (to_mate(target_at(s)).start(), z)[1], 0)
    to_sibling(u).start()

    for step in range(1, pairs):
        v = lax.rem(u + step, pairs)
        to_sibling(v).wait_recv()
        to_far[v] = (np_ref[v * 2 + c].astype(f32) + from_sib[v].astype(f32)).astype(bf16)
        to_other(v, u).start()

    def pass_on(s, z):
        q = target_at(s)
        to_mate(q).wait_recv()

        @pl.when(jnp.logical_and(q >= p, has_left))
        def _():
            along(q, 0, right).wait_recv()

        @pl.when(jnp.logical_and(q <= p, has_right))
        def _():
            along(q, 1, left).wait_recv()

        def own():
            return wp_ref[q * 2 + x].astype(f32) + from_mate[q].astype(f32)

        @pl.when(q > p)
        def _():
            @pl.when(has_left)
            def _():
                to_line[q] = (own() + from_line[0, q].astype(f32)).astype(bf16)

            @pl.when(jnp.logical_not(has_left))
            def _():
                to_line[q] = own().astype(bf16)

            along(q, 0, right).start()

        @pl.when(q < p)
        def _():
            @pl.when(has_right)
            def _():
                to_line[q] = (own() + from_line[1, q].astype(f32)).astype(bf16)

            @pl.when(jnp.logical_not(has_right))
            def _():
                to_line[q] = own().astype(bf16)

            along(q, 1, left).start()

        return z

    lax.fori_loop(0, line - 1, pass_on, 0)

    to_sibling(u).wait_recv()
    total = np_ref[f].astype(f32) + from_sib[u].astype(f32)
    for step in range(1, pairs):
        v = lax.rem(u + step, pairs)
        to_other(v, v).wait_recv()
        total = total + from_far[v].astype(f32)
    rows = h_ref[...].astype(f32)
    mean_row = jnp.mean(rows, axis=-1, keepdims=True)
    centered = rows - mean_row
    inv_std = lax.rsqrt(jnp.mean(centered * centered, axis=-1, keepdims=True) + norm_eps)
    gain = gain_ref[...].reshape(1, -1)
    hout_ref[...] = norm_backward(total, centered * inv_std, inv_std, gain)

    pass_on(line - 1, 0)
    zero = jnp.zeros(wp_ref.shape[1:], f32)

    @pl.when(jnp.logical_not(has_left))
    def _():
        from_line[0, p] = zero.astype(bf16)

    @pl.when(jnp.logical_not(has_right))
    def _():
        from_line[1, p] = zero.astype(bf16)

    final = wp_ref[i].astype(f32) + from_mate[p].astype(f32)
    final = final + from_line[0, p].astype(f32) + from_line[1, p].astype(f32)
    wout_ref[...] = final

    def sent(q, z):
        to_mate(q).wait_send()

        @pl.when(q != p)
        def _():
            along(q, 0, right).wait_send()

        return z

    lax.fori_loop(0, line, sent, 0)
    for v in range(pairs):
        to_sibling(v).wait_send()
    for step in range(1, pairs):
        v = lax.rem(u + step, pairs)
        to_other(v, u).wait_send()


def reduce_all(dp, frames, weight_part, norm_part, hidden, gain):
    dma = pltpu.SemaphoreType.DMA
    vmem = pl.BlockSpec(memory_space=pltpu.VMEM)
    pairs, line = frames // 2, dp // 2
    bf16, f32 = jnp.bfloat16, jnp.float32
    own_rows, cols = weight_part.shape[1:]
    moved = 2 * (weight_part.size + norm_part.size)
    return pl.pallas_call(
        functools.partial(reduce_kernel, dp, frames),
        out_shape=(
            jax.ShapeDtypeStruct((own_rows, cols), f32),
            jax.ShapeDtypeStruct(hidden.shape, bf16),
        ),
        in_specs=[vmem] * 4,
        out_specs=(vmem,) * 2,
        scratch_shapes=[
            pltpu.VMEM((line, own_rows, cols), bf16),
            pltpu.VMEM((2, line, own_rows, cols), bf16),
            pltpu.VMEM((line, own_rows, cols), bf16),
            pltpu.VMEM((pairs,) + hidden.shape, bf16),
            pltpu.VMEM((pairs,) + hidden.shape, bf16),
            pltpu.VMEM((pairs,) + hidden.shape, bf16),
            dma((line,)), dma((line,)), dma((line,)), dma((2, line)),
            dma((pairs,)), dma((pairs,)), dma((pairs,)), dma((pairs,)),
        ],
        compiler_params=pltpu.CompilerParams(
            collective_id=1, has_side_effects=True, vmem_limit_bytes=VMEM_LIMIT
        ),
        cost_estimate=pl.CostEstimate(flops=0, bytes_accessed=10 * moved, transcendentals=0),
        name="reduce_all",
    )(weight_part, norm_part, hidden, gain)


def per_device(
    hidden_in, rec_lengths, token_positions, thinker_grad, norm_gain, norm_bias, qkv_weight
):
    frame_count = lax.axis_size("frame")
    dp_count = lax.axis_size("dp")
    own_rows, three, head_cols = qkv_weight.shape
    heads = head_cols // HD
    own_frames, width = hidden_in.shape
    group_frames = token_positions.shape[0]
    think_rows = thinker_grad.shape[0]
    parts = (heads // 2, heads - heads // 2)
    first_own, second_own = part_weight(qkv_weight.transpose(1, 0, 2), parts)
    second_weight = lax.all_gather(second_own, "dp", axis=0, tiled=True)
    first_weight, group_norm, moved = gather_all(
        dp_count, frame_count, first_own, hidden_in, norm_gain, norm_bias, thinker_grad
    )
    first_weight = first_weight.reshape(width, first_own.shape[1])
    group_norm = group_norm.reshape(group_frames, width)
    out_grad, first_grad, first_part = local_work(
        True, rec_lengths, group_norm, first_weight,
        token_positions.reshape(1, group_frames),
        moved.reshape(frame_count * think_rows, head_cols),
    )
    first_total = lax.psum_scatter(first_part, "dp", scatter_dimension=0, tiled=True)
    norm_part, second_part = local_work(
        False, rec_lengths, group_norm, second_weight, out_grad, first_grad, first_weight
    )
    second_total, hidden_grad = reduce_all(
        dp_count, frame_count,
        second_part.reshape(dp_count, own_rows, second_part.shape[1]),
        norm_part.reshape(frame_count, own_frames, width),
        hidden_in, norm_gain,
    )
    weight_grad, hidden_grad = finish(first_total, second_total, hidden_grad)
    return (hidden_grad, weight_grad.transpose(1, 0, 2))


def solution(mesh):
    placed = (
        P(("dp", "frame"), None),
        P("dp", None),
        P("dp"),
        P(("dp", "frame"), None),
        P(),
        P(),
        P("dp", None, "frame"),
    )
    return jax.shard_map(
        per_device,
        mesh=mesh,
        in_specs=placed,
        out_specs=(P(("dp", "frame"), None), P("dp", None, "frame")),
        check_vma=False,
    )
```

```python
import functools
import math

import jax
import jax.numpy as jnp
from jax import lax
from jax.experimental import pallas as pl
from jax.experimental.pallas import tpu as pltpu
from jax.sharding import PartitionSpec as P

HD = 64
MESH = pl.DeviceIdType.MESH
VMEM_LIMIT = 56 * 1024 * 1024

norm_eps = 1e-05
NEG = -1e30


def norm_forward(rows, gain, bias):
    rows_f32 = rows.astype(jnp.float32)
    mean_row = jnp.mean(rows_f32, axis=-1, keepdims=True)
    centered = rows_f32 - mean_row
    variance = jnp.mean(centered * centered, axis=-1, keepdims=True)
    inv_std = lax.rsqrt(variance + norm_eps)
    standard = centered * inv_std
    normalized = (standard * gain + bias).astype(jnp.bfloat16)
    return (normalized, standard, inv_std)


def norm_backward(norm_grad, standard, inv_std, gain):
    scaled = norm_grad * gain
    result = inv_std * (
        scaled
        - jnp.mean(scaled, axis=-1, keepdims=True)
        - standard * jnp.mean(scaled * standard, axis=-1, keepdims=True)
    )
    return result.astype(jnp.bfloat16)


def gather_kernel(
    dp, frames, w_in, h_in, gain_ref, bias_ref, t_in, wg_ref, ng_ref, tg_ref,
    w_ref, n_ref, t_ref, w_send, w_recv, n_send, n_recv, t_send, t_recv, own_sem,
):
    head_cols = w_in.shape[2]
    line = dp // 2
    pairs = frames // 2
    i = lax.axis_index("dp")
    f = lax.axis_index("frame")
    x, p = lax.rem(i, 2), lax.div(i, 2)
    c, u = lax.rem(f, 2), lax.div(f, 2)
    mate = p * 2 + (1 - x)
    right, left = i + 2, i - 2
    has_right, has_left = p < line - 1, p > 0

    barrier = pltpu.get_barrier_semaphore()
    pl.semaphore_signal(barrier, inc=1, device_id=(mate, f), device_id_type=MESH)

    @pl.when(has_right)
    def _():
        pl.semaphore_signal(barrier, inc=1, device_id=(right, f), device_id_type=MESH)

    @pl.when(has_left)
    def _():
        pl.semaphore_signal(barrier, inc=1, device_id=(left, f), device_id_type=MESH)

    for step in range(1, frames):
        other = lax.rem(f + step, frames)
        pl.semaphore_signal(barrier, inc=1, device_id=(i, other), device_id_type=MESH)
    for h in range(head_cols // HD):
        for kind in range(3):
            at = (3 * h + kind) * HD
            w_ref[:, at:at + HD] = w_in[kind, :, h * HD:(h + 1) * HD]

    ends = jnp.where(has_right, 1, 0) + jnp.where(has_left, 1, 0)
    pl.semaphore_wait(barrier, frames + ends)

    def w_copy(src, slot, way, target):
        return pltpu.make_async_remote_copy(
            src_ref=src, dst_ref=wg_ref.at[slot],
            send_sem=w_send.at[way, slot], recv_sem=w_recv.at[slot],
            device_id=(target, f), device_id_type=MESH,
        )

    def n_copy(src, slot, way, target):
        return pltpu.make_async_remote_copy(
            src_ref=src, dst_ref=ng_ref.at[slot],
            send_sem=n_send.at[way, slot], recv_sem=n_recv.at[slot],
            device_id=(i, target), device_id_type=MESH,
        )

    def t_copy(target):
        return pltpu.make_async_remote_copy(
            src_ref=t_ref.at[target], dst_ref=tg_ref.at[f],
            send_sem=t_send.at[target], recv_sem=t_recv.at[f],
            device_id=(i, target), device_id_type=MESH,
        )

    @pl.when(has_right)
    def _():
        w_copy(w_ref, i, 0, right).start()

    @pl.when(has_left)
    def _():
        w_copy(w_ref, i, 1, left).start()

    w_copy(w_ref, i, 2, mate).start()
    sibling = u * 2 + (1 - c)
    n_ref[...] = norm_forward(
        h_in[...], gain_ref[...].reshape(1, -1), bias_ref[...].reshape(1, -1)
    )[0]
    for step in range(1, pairs):
        far = lax.rem(u + step, pairs) * 2 + c
        n_copy(n_ref, f, step, far).start()
    n_copy(n_ref, f, 0, sibling).start()
    for target in range(frames):
        t_ref[target] = t_in[:, target * head_cols:(target + 1) * head_cols]
    for step in range(1, frames):
        t_copy(lax.rem(f + step, frames)).start()
    own_w = pltpu.make_async_copy(w_ref, wg_ref.at[i], own_sem.at[0])
    own_n = pltpu.make_async_copy(n_ref, ng_ref.at[f], own_sem.at[1])
    own_t = pltpu.make_async_copy(t_ref.at[f], tg_ref.at[f], own_sem.at[2])
    own_w.start()
    own_n.start()
    own_t.start()

    def relay(step):
        from_left = i - 2 * step
        from_right = i + 2 * step

        @pl.when(p - step >= 0)
        def _():
            w_copy(w_ref, from_left, 0, mate).wait_recv()

            @pl.when(has_right)
            def _():
                w_copy(wg_ref.at[from_left], from_left, 0, right).start()

            w_copy(wg_ref.at[from_left], from_left, 2, mate).start()

        @pl.when(p + step <= line - 1)
        def _():
            w_copy(w_ref, from_right, 1, mate).wait_recv()

            @pl.when(has_left)
            def _():
                w_copy(wg_ref.at[from_right], from_right, 1, left).start()

            w_copy(wg_ref.at[from_right], from_right, 2, mate).start()

    def relay_norm():
        for step in range(1, pairs):
            far = lax.rem(u + step, pairs) * 2 + c
            n_copy(n_ref, far, 0, sibling).wait_recv()
            n_copy(ng_ref.at[far], far, 0, sibling).start()

    for step in range(1, min(line, 3)):
        relay(step)
    relay_norm()
    if line > 3:
        lax.fori_loop(3, line, lambda s, z: (relay(s), z)[1], 0)

    def finish(q, z):
        w_copy(w_ref, q * 2 + (1 - x), 2, mate).wait_recv()
        w_copy(w_ref, q * 2 + x, 2, mate).wait_send()

        @pl.when(jnp.logical_and(q <= p, has_right))
        def _():
            w_copy(w_ref, q * 2 + x, 0, right).wait_send()

        @pl.when(jnp.logical_and(q >= p, has_left))
        def _():
            w_copy(w_ref, q * 2 + x, 1, left).wait_send()

        return z

    for step in range(1, pairs):
        far = lax.rem(u + step, pairs) * 2 + c
        n_copy(n_ref, f, step, far).wait_send()
        n_copy(n_ref, far, 0, sibling).wait_send()
    n_copy(n_ref, f, 0, sibling).wait_send()
    for v in range(pairs):
        n_copy(n_ref, v * 2 + (1 - c), 0, sibling).wait_recv()
    for step in range(1, frames):
        other = lax.rem(f + step, frames)
        t_copy(other).wait_send()
        pltpu.make_async_remote_copy(
            src_ref=t_ref.at[other], dst_ref=tg_ref.at[other],
            send_sem=t_send.at[other], recv_sem=t_recv.at[other],
            device_id=(i, other), device_id_type=MESH,
        ).wait_recv()
    lax.fori_loop(0, line, finish, 0)
    own_w.wait()
    own_n.wait()
    own_t.wait()


def gather_all(dp, frames, weight, hidden, gain, bias, thinker):
    dma = pltpu.SemaphoreType.DMA
    any_spec = pl.BlockSpec(memory_space=pl.ANY)
    vmem = pl.BlockSpec(memory_space=pltpu.VMEM)
    pairs = frames // 2
    kinds, own_rows, head_cols = weight.shape
    think_rows = thinker.shape[0]
    w_own = (own_rows, kinds * head_cols)
    t_own = (frames, think_rows, head_cols)
    moved = 2 * (dp * weight.size + frames * hidden.size + thinker.size)
    return pl.pallas_call(
        functools.partial(gather_kernel, dp, frames),
        out_shape=(
            jax.ShapeDtypeStruct((dp,) + w_own, weight.dtype),
            jax.ShapeDtypeStruct((frames,) + hidden.shape, hidden.dtype),
            jax.ShapeDtypeStruct(t_own, thinker.dtype),
        ),
        in_specs=[vmem] * 5,
        out_specs=(any_spec,) * 3,
        scratch_shapes=[
            pltpu.VMEM(w_own, weight.dtype),
            pltpu.VMEM(hidden.shape, hidden.dtype),
            pltpu.VMEM(t_own, thinker.dtype),
            dma((3, dp)), dma((dp,)),
            dma((pairs, frames)), dma((frames,)),
            dma((frames,)), dma((frames,)),
            dma((3,)),
        ],
        compiler_params=pltpu.CompilerParams(
            collective_id=0, has_side_effects=True, vmem_limit_bytes=VMEM_LIMIT
        ),
        cost_estimate=pl.CostEstimate(flops=0, bytes_accessed=2 * moved, transcendentals=0),
        name="gather_all",
    )(weight, hidden, gain, bias, thinker)


def local_kernel(
    rows_tile, tile_q, windows, len_ref, pos_ref, n_ref, w_ref, t_ref, ng_ref, wp_ref,
    q_s, k_s, v_s, g_s, kt_s, dq_s, dk_s, dv_s, dk_acc, dv_acc, grad_s,
):
    length, width = n_ref.shape
    cols = w_ref.shape[1]
    heads = cols // (3 * HD)
    recs = len_ref.shape[1]
    slack = t_ref.shape[0] - length
    scale = HD ** (-0.5)
    expo_scale = scale * math.log2(math.e)

    ends = []
    total = 0
    for r in range(recs):
        total = total + len_ref[0, r]
        ends.append(total)

    @pl.loop(0, length // rows_tile)
    def _(t):
        r0 = pl.multiple_of(t * rows_tile, rows_tile)
        rows = pl.ds(r0, rows_tile)
        proj = jnp.dot(n_ref[rows, :], w_ref[...], preferred_element_type=jnp.float32)
        proj = proj.astype(jnp.bfloat16)
        frame_ids = r0 + lax.broadcasted_iota(jnp.int32, (rows_tile, HD), 0)
        lane = lax.broadcasted_iota(jnp.int32, (rows_tile, HD), 1)
        seg = jnp.zeros((rows_tile, HD), jnp.int32)
        for end in ends:
            seg = seg + jnp.where(frame_ids >= end, 1, 0)
        same = seg == lane
        q_mask = jnp.where(jnp.logical_or(same, lane >= recs), 0.0, NEG).astype(jnp.bfloat16)
        k_mask = jnp.where(same, 1.0, 0.0).astype(jnp.bfloat16)
        cover = rows_tile + slack
        col = r0 + lax.broadcasted_iota(jnp.int32, (rows_tile, cover), 1)
        places = jnp.broadcast_to(pos_ref[:, rows], (128, rows_tile)).T[:, 0:1]
        pick = jnp.where(col == places, 1.0, 0.0).astype(jnp.bfloat16)
        out_grad = jnp.dot(
            pick, t_ref[pl.ds(r0, cover), :], preferred_element_type=jnp.float32
        ).astype(jnp.bfloat16)
        for h in range(heads):
            base = 3 * HD * h
            keys = proj[:, base + HD:base + 2 * HD]
            q_s[h, rows, 0:HD] = proj[:, base:base + HD]
            q_s[h, rows, HD:2 * HD] = q_mask
            k_s[h, rows, 0:HD] = keys
            k_s[h, rows, HD:2 * HD] = k_mask
            kt_s[h, :, rows] = keys.T
            v_s[h, rows, :] = proj[:, base + 2 * HD:base + 3 * HD]
            g_s[h, rows, :] = out_grad[:, h * HD:(h + 1) * HD]

    tiles = length // tile_q
    nt = (((1,), (1,)), ((), ()))

    dk_acc[...] = jnp.zeros_like(dk_acc)
    dv_acc[...] = jnp.zeros_like(dv_acc)

    @pl.loop(0, tiles)
    def _(t):
        q0 = pl.multiple_of(t * tile_q, tile_q)
        q_last = q0 + tile_q - 1
        q_span = pl.ds(q0, tile_q)
        low = jnp.int32(0)
        high = jnp.int32(length)
        for end in ends:
            low = jnp.where(end <= q0, jnp.maximum(low, end), low)
            high = jnp.where(end > q_last, jnp.minimum(high, end), high)
        low = (low // 128) * 128
        need = high - low

        def attend(window):
            start = pl.multiple_of(jnp.minimum(low, length - window), 128)
            span = pl.ds(start, window)

            def products(h):
                scores = lax.dot_general(
                    k_s[h, span, :], q_s[h, q_span, :], nt, preferred_element_type=jnp.float32
                )
                grads = lax.dot_general(
                    v_s[h, span, :], g_s[h, q_span, :], nt, preferred_element_type=jnp.float32
                )
                return scores, grads

            def softmax_grads(scores, grads):
                top = jnp.max(scores, axis=0, keepdims=True)
                expo = jnp.exp2((scores - top) * expo_scale)
                weights = expo * (1.0 / jnp.sum(expo, axis=0, keepdims=True))
                row_dot = jnp.sum(weights * grads, axis=0, keepdims=True)
                score_grad = (weights * (grads - row_dot)).astype(jnp.bfloat16)
                return weights.astype(jnp.bfloat16), score_grad

            def accumulate(h, weights, score_grad):
                dv_acc[h, span, :] += jnp.dot(
                    weights, g_s[h, q_span, :], preferred_element_type=jnp.float32
                )
                dk_acc[h, span, :] += jnp.dot(
                    score_grad, q_s[h, q_span, 0:HD], preferred_element_type=jnp.float32
                )
                dq_t = jnp.dot(kt_s[h, :, span], score_grad, preferred_element_type=jnp.float32)
                dq_s[h, q_span, :] = (dq_t * scale).T.astype(jnp.bfloat16)

            ahead = products(0)
            for h in range(heads):
                now = ahead
                if h + 1 < heads:
                    ahead = products(h + 1)
                accumulate(h, *softmax_grads(*now))

        smaller = 0
        for window in windows:
            @pl.when(jnp.logical_and(need > smaller, need <= window))
            def _(window=window):
                attend(window)
            smaller = window

    for h in range(heads):
        dk_s[h] = (dk_acc[h] * scale).astype(jnp.bfloat16)
        dv_s[h] = dv_acc[h].astype(jnp.bfloat16)

    @pl.loop(0, length // rows_tile)
    def _(t):
        rows = pl.ds(pl.multiple_of(t * rows_tile, rows_tile), rows_tile)
        parts = []
        for h in range(heads):
            parts += [dq_s[h, rows, :], dk_s[h, rows, :], dv_s[h, rows, :]]
        grad = jnp.concatenate(parts, axis=1)
        grad_s[rows, :] = grad
        ng_ref[rows, :] = lax.dot_general(
            grad, w_ref[...], nt, preferred_element_type=jnp.float32
        ).astype(jnp.bfloat16)

    @pl.loop(0, width // rows_tile)
    def _(t):
        rows = pl.ds(pl.multiple_of(t * rows_tile, rows_tile), rows_tile)
        wp_ref[rows, :] = lax.dot_general(
            n_ref[:, rows], grad_s[...], (((0,), (0,)), ((), ())),
            preferred_element_type=jnp.float32,
        ).astype(jnp.bfloat16)


def local_work(lengths, positions, group_norm, weight, thinker):
    length, width = group_norm.shape
    cols = weight.shape[1]
    heads = cols // (3 * HD)
    rows_tile = 256
    tile_q = 256
    windows = tuple(w for w in (512, 768) if w < length) + (length,)
    vmem = pl.BlockSpec(memory_space=pltpu.VMEM)
    bf16, f32 = jnp.bfloat16, jnp.float32
    return pl.pallas_call(
        functools.partial(local_kernel, rows_tile, tile_q, windows),
        out_shape=(
            jax.ShapeDtypeStruct((length, width), bf16),
            jax.ShapeDtypeStruct((width, cols), bf16),
        ),
        in_specs=[pl.BlockSpec(memory_space=pltpu.SMEM)] + [vmem] * 4,
        out_specs=(vmem, vmem),
        scratch_shapes=[
            pltpu.VMEM((heads, length, 2 * HD), bf16),
            pltpu.VMEM((heads, length, 2 * HD), bf16),
            pltpu.VMEM((heads, length, HD), bf16),
            pltpu.VMEM((heads, length, HD), bf16),
            pltpu.VMEM((heads, HD, length), bf16),
            pltpu.VMEM((heads, length, HD), bf16),
            pltpu.VMEM((heads, length, HD), bf16),
            pltpu.VMEM((heads, length, HD), bf16),
            pltpu.VMEM((heads, length, HD), f32),
            pltpu.VMEM((heads, length, HD), f32),
            pltpu.VMEM((length, cols), bf16),
        ],
        compiler_params=pltpu.CompilerParams(vmem_limit_bytes=VMEM_LIMIT),
        name="local_work",
    )(lengths, positions, group_norm, weight, thinker)


def reduce_kernel(
    dp, frames, wp_ref, np_ref, h_ref, gain_ref, wout_ref, hout_ref,
    own_w, own_n, from_mate, from_line, to_line, from_sib, from_far, to_far,
    m_send, m_recv, l_send, l_recv, s_send, s_recv, f_send, f_recv, w_sem, n_sem,
):
    line = dp // 2
    pairs = frames // 2
    i = lax.axis_index("dp")
    f = lax.axis_index("frame")
    x, p = lax.rem(i, 2), lax.div(i, 2)
    c, u = lax.rem(f, 2), lax.div(f, 2)
    mate = p * 2 + (1 - x)
    right, left = i + 2, i - 2
    has_right, has_left = p < line - 1, p > 0
    sibling = u * 2 + (1 - c)
    f32, bf16 = jnp.float32, jnp.bfloat16

    def load_w(q):
        return pltpu.make_async_copy(wp_ref.at[q * 2 + x], own_w.at[q], w_sem.at[q])

    def load_n(v):
        return pltpu.make_async_copy(np_ref.at[v * 2 + c], own_n.at[v], n_sem.at[v])

    barrier = pltpu.get_barrier_semaphore()
    pl.semaphore_signal(barrier, inc=1, device_id=(mate, f), device_id_type=MESH)

    @pl.when(has_right)
    def _():
        pl.semaphore_signal(barrier, inc=1, device_id=(right, f), device_id_type=MESH)

    @pl.when(has_left)
    def _():
        pl.semaphore_signal(barrier, inc=1, device_id=(left, f), device_id_type=MESH)

    pl.semaphore_signal(barrier, inc=1, device_id=(i, sibling), device_id_type=MESH)
    for step in range(1, pairs):
        far = lax.rem(u + step, pairs) * 2 + c
        pl.semaphore_signal(barrier, inc=1, device_id=(i, far), device_id_type=MESH)
    ends = jnp.where(has_right, 1, 0) + jnp.where(has_left, 1, 0)
    pl.semaphore_wait(barrier, 1 + pairs + ends)

    def to_mate(q):
        return pltpu.make_async_remote_copy(
            src_ref=wp_ref.at[q * 2 + (1 - x)], dst_ref=from_mate.at[q],
            send_sem=m_send.at[q], recv_sem=m_recv.at[q],
            device_id=(mate, f), device_id_type=MESH,
        )

    def along(q, way, target):
        return pltpu.make_async_remote_copy(
            src_ref=to_line.at[q], dst_ref=from_line.at[way, q],
            send_sem=l_send.at[q], recv_sem=l_recv.at[way, q],
            device_id=(target, f), device_id_type=MESH,
        )

    def to_sibling(v):
        return pltpu.make_async_remote_copy(
            src_ref=np_ref.at[v * 2 + (1 - c)], dst_ref=from_sib.at[v],
            send_sem=s_send.at[v], recv_sem=s_recv.at[v],
            device_id=(i, sibling), device_id_type=MESH,
        )

    def to_other(v, slot):
        return pltpu.make_async_remote_copy(
            src_ref=to_far.at[v], dst_ref=from_far.at[slot],
            send_sem=f_send.at[v], recv_sem=f_recv.at[slot],
            device_id=(i, v * 2 + c), device_id_type=MESH,
        )

    ahead, behind = line - 1 - p, p

    def target_at(s):
        lower = jnp.where(s < ahead, line - 1 - s, s - ahead)
        upper = jnp.where(s < behind, s, line - 1 - (s - behind))
        return jnp.where(p < line // 2, lower, upper)

    for step in range(1, pairs):
        to_sibling(lax.rem(u + step, pairs)).start()
    lax.fori_loop(0, line, lambda s, z: (to_mate(target_at(s)).start(), z)[1], 0)
    to_sibling(u).start()

    for v in range(pairs):
        load_n(v).start()
    lax.fori_loop(0, line, lambda s, z: (load_w(target_at(s)).start(), z)[1], 0)

    for step in range(1, pairs):
        v = lax.rem(u + step, pairs)
        load_n(v).wait()
        to_sibling(v).wait_recv()
        to_far[v] = (own_n[v].astype(f32) + from_sib[v].astype(f32)).astype(bf16)
        to_other(v, u).start()

    def pass_on(s, z):
        q = target_at(s)
        load_w(q).wait()
        to_mate(q).wait_recv()

        @pl.when(jnp.logical_and(q >= p, has_left))
        def _():
            along(q, 0, right).wait_recv()

        @pl.when(jnp.logical_and(q <= p, has_right))
        def _():
            along(q, 1, left).wait_recv()

        def own():
            return own_w[q].astype(f32) + from_mate[q].astype(f32)

        @pl.when(q > p)
        def _():
            @pl.when(has_left)
            def _():
                to_line[q] = (own() + from_line[0, q].astype(f32)).astype(bf16)

            @pl.when(jnp.logical_not(has_left))
            def _():
                to_line[q] = own().astype(bf16)

            along(q, 0, right).start()

        @pl.when(q < p)
        def _():
            @pl.when(has_right)
            def _():
                to_line[q] = (own() + from_line[1, q].astype(f32)).astype(bf16)

            @pl.when(jnp.logical_not(has_right))
            def _():
                to_line[q] = own().astype(bf16)

            along(q, 1, left).start()

        return z

    lax.fori_loop(0, line - 1, pass_on, 0)

    load_n(u).wait()
    to_sibling(u).wait_recv()
    total = own_n[u].astype(f32) + from_sib[u].astype(f32)
    for step in range(1, pairs):
        v = lax.rem(u + step, pairs)
        to_other(v, v).wait_recv()
        total = total + from_far[v].astype(f32)
    rows = h_ref[...].astype(f32)
    mean_row = jnp.mean(rows, axis=-1, keepdims=True)
    centered = rows - mean_row
    inv_std = lax.rsqrt(jnp.mean(centered * centered, axis=-1, keepdims=True) + norm_eps)
    gain = gain_ref[...].reshape(1, -1)
    hout_ref[...] = norm_backward(total, centered * inv_std, inv_std, gain)

    pass_on(line - 1, 0)
    zero = jnp.zeros(wp_ref.shape[1:], f32)

    @pl.when(jnp.logical_not(has_left))
    def _():
        from_line[0, p] = zero.astype(bf16)

    @pl.when(jnp.logical_not(has_right))
    def _():
        from_line[1, p] = zero.astype(bf16)

    final = own_w[p].astype(f32) + from_mate[p].astype(f32)
    final = final + from_line[0, p].astype(f32) + from_line[1, p].astype(f32)
    wout_ref[...] = final

    def sent(q, z):
        to_mate(q).wait_send()

        @pl.when(q != p)
        def _():
            along(q, 0, right).wait_send()

        return z

    lax.fori_loop(0, line, sent, 0)
    for v in range(pairs):
        to_sibling(v).wait_send()
    for step in range(1, pairs):
        v = lax.rem(u + step, pairs)
        to_other(v, u).wait_send()


def reduce_all(dp, frames, weight_part, norm_part, hidden, gain):
    dma = pltpu.SemaphoreType.DMA
    vmem = pl.BlockSpec(memory_space=pltpu.VMEM)
    pairs, line = frames // 2, dp // 2
    bf16, f32 = jnp.bfloat16, jnp.float32
    own_rows, cols = weight_part.shape[1:]
    moved = 2 * (weight_part.size + norm_part.size)
    return pl.pallas_call(
        functools.partial(reduce_kernel, dp, frames),
        out_shape=(
            jax.ShapeDtypeStruct((own_rows, cols), f32),
            jax.ShapeDtypeStruct(hidden.shape, bf16),
        ),
        in_specs=[pl.BlockSpec(memory_space=pl.ANY)] * 2 + [vmem] * 2,
        out_specs=(vmem,) * 2,
        scratch_shapes=[
            pltpu.VMEM((line, own_rows, cols), bf16),
            pltpu.VMEM((pairs,) + hidden.shape, bf16),
            pltpu.VMEM((line, own_rows, cols), bf16),
            pltpu.VMEM((2, line, own_rows, cols), bf16),
            pltpu.VMEM((line, own_rows, cols), bf16),
            pltpu.VMEM((pairs,) + hidden.shape, bf16),
            pltpu.VMEM((pairs,) + hidden.shape, bf16),
            pltpu.VMEM((pairs,) + hidden.shape, bf16),
            dma((line,)), dma((line,)), dma((line,)), dma((2, line)),
            dma((pairs,)), dma((pairs,)), dma((pairs,)), dma((pairs,)),
            dma((line,)), dma((pairs,)),
        ],
        compiler_params=pltpu.CompilerParams(
            collective_id=1, has_side_effects=True, vmem_limit_bytes=VMEM_LIMIT
        ),
        cost_estimate=pl.CostEstimate(flops=0, bytes_accessed=2 * moved, transcendentals=0),
        name="reduce_all",
    )(weight_part, norm_part, hidden, gain)


def finish_kernel(w_ref, h_ref, w_out, h_out):
    for h in range(w_out.shape[2] // HD):
        for kind in range(3):
            at = (3 * h + kind) * HD
            w_out[kind, :, h * HD:(h + 1) * HD] = w_ref[:, at:at + HD]
    h_out[...] = h_ref[...]


def finish(weight_grad, hidden_grad):
    vmem = pl.BlockSpec(memory_space=pltpu.VMEM)
    rows, cols = weight_grad.shape
    return pl.pallas_call(
        finish_kernel,
        out_shape=(
            jax.ShapeDtypeStruct((3, rows, cols // 3), jnp.float32),
            jax.ShapeDtypeStruct(hidden_grad.shape, hidden_grad.dtype),
        ),
        in_specs=[vmem] * 2,
        out_specs=(vmem,) * 2,
        name="finish",
    )(weight_grad, hidden_grad)


def per_device(
    hidden_in, rec_lengths, token_positions, thinker_grad, norm_gain, norm_bias, qkv_weight
):
    frame_count = lax.axis_size("frame")
    dp_count = lax.axis_size("dp")
    own_rows, three, head_cols = qkv_weight.shape
    heads = head_cols // HD
    own_frames, width = hidden_in.shape
    group_frames = token_positions.shape[0]
    think_rows = thinker_grad.shape[0]
    weight, group_norm, moved = gather_all(
        dp_count, frame_count, qkv_weight.transpose(1, 0, 2), hidden_in,
        norm_gain, norm_bias, thinker_grad,
    )
    norm_part, weight_part = local_work(
        rec_lengths,
        token_positions.reshape(1, group_frames),
        group_norm.reshape(group_frames, width),
        weight.reshape(width, 3 * head_cols),
        moved.reshape(frame_count * think_rows, head_cols),
    )
    weight_total, hidden_grad = reduce_all(
        dp_count, frame_count,
        weight_part.reshape(dp_count, own_rows, 3 * head_cols),
        norm_part.reshape(frame_count, own_frames, width),
        hidden_in, norm_gain,
    )
    weight_grad, hidden_grad = finish(weight_total, hidden_grad)
    return (hidden_grad, weight_grad.transpose(1, 0, 2))


def solution(mesh):
    placed = (
        P(("dp", "frame"), None),
        P("dp", None),
        P("dp"),
        P(("dp", "frame"), None),
        P(),
        P(),
        P("dp", None, "frame"),
    )
    return jax.shard_map(
        per_device,
        mesh=mesh,
        in_specs=placed,
        out_specs=(P(("dp", "frame"), None), P("dp", None, "frame")),
        check_vma=False,
    )
```

```python
import functools
import math

import jax
import jax.numpy as jnp
from jax import lax
from jax.experimental import pallas as pl
from jax.experimental.pallas import tpu as pltpu
from jax.sharding import PartitionSpec as P

HD = 64
MESH = pl.DeviceIdType.MESH
VMEM_LIMIT = 56 * 1024 * 1024

norm_eps = 1e-05
NEG = -1e30


def norm_forward(rows, gain, bias):
    rows_f32 = rows.astype(jnp.float32)
    mean_row = jnp.mean(rows_f32, axis=-1, keepdims=True)
    centered = rows_f32 - mean_row
    variance = jnp.mean(centered * centered, axis=-1, keepdims=True)
    inv_std = lax.rsqrt(variance + norm_eps)
    standard = centered * inv_std
    normalized = (standard * gain + bias).astype(jnp.bfloat16)
    return (normalized, standard, inv_std)


def norm_backward(norm_grad, standard, inv_std, gain):
    scaled = norm_grad * gain
    result = inv_std * (
        scaled
        - jnp.mean(scaled, axis=-1, keepdims=True)
        - standard * jnp.mean(scaled * standard, axis=-1, keepdims=True)
    )
    return result.astype(jnp.bfloat16)


def gather_kernel(
    dp, frames, w_in, h_in, gain_ref, bias_ref, t_in, wg_ref, ng_ref, tg_ref,
    w_ref, n_ref, t_ref, w_send, w_recv, n_send, n_recv, t_send, t_recv, own_sem,
):
    head_cols = w_in.shape[2]
    line = dp // 2
    pairs = frames // 2
    i = lax.axis_index("dp")
    f = lax.axis_index("frame")
    x, p = lax.rem(i, 2), lax.div(i, 2)
    c, u = lax.rem(f, 2), lax.div(f, 2)
    mate = p * 2 + (1 - x)
    right, left = i + 2, i - 2
    has_right, has_left = p < line - 1, p > 0

    barrier = pltpu.get_barrier_semaphore()
    pl.semaphore_signal(barrier, inc=1, device_id=(mate, f), device_id_type=MESH)

    @pl.when(has_right)
    def _():
        pl.semaphore_signal(barrier, inc=1, device_id=(right, f), device_id_type=MESH)

    @pl.when(has_left)
    def _():
        pl.semaphore_signal(barrier, inc=1, device_id=(left, f), device_id_type=MESH)

    for step in range(1, frames):
        other = lax.rem(f + step, frames)
        pl.semaphore_signal(barrier, inc=1, device_id=(i, other), device_id_type=MESH)
    for h in range(head_cols // HD):
        for kind in range(3):
            at = (3 * h + kind) * HD
            w_ref[:, at:at + HD] = w_in[kind, :, h * HD:(h + 1) * HD]

    ends = jnp.where(has_right, 1, 0) + jnp.where(has_left, 1, 0)
    pl.semaphore_wait(barrier, frames + ends)

    def w_copy(src, slot, way, target):
        return pltpu.make_async_remote_copy(
            src_ref=src, dst_ref=wg_ref.at[slot],
            send_sem=w_send.at[way, slot], recv_sem=w_recv.at[slot],
            device_id=(target, f), device_id_type=MESH,
        )

    def n_copy(src, slot, way, target):
        return pltpu.make_async_remote_copy(
            src_ref=src, dst_ref=ng_ref.at[slot],
            send_sem=n_send.at[way, slot], recv_sem=n_recv.at[slot],
            device_id=(i, target), device_id_type=MESH,
        )

    def t_copy(target):
        return pltpu.make_async_remote_copy(
            src_ref=t_ref.at[target], dst_ref=tg_ref.at[f],
            send_sem=t_send.at[target], recv_sem=t_recv.at[f],
            device_id=(i, target), device_id_type=MESH,
        )

    @pl.when(has_right)
    def _():
        w_copy(w_ref, i, 0, right).start()

    @pl.when(has_left)
    def _():
        w_copy(w_ref, i, 1, left).start()

    w_copy(w_ref, i, 2, mate).start()
    sibling = u * 2 + (1 - c)
    n_ref[...] = norm_forward(
        h_in[...], gain_ref[...].reshape(1, -1), bias_ref[...].reshape(1, -1)
    )[0]
    for step in range(1, pairs):
        far = lax.rem(u + step, pairs) * 2 + c
        n_copy(n_ref, f, step, far).start()
    n_copy(n_ref, f, 0, sibling).start()
    for target in range(frames):
        t_ref[target] = t_in[:, target * head_cols:(target + 1) * head_cols]
    for step in range(1, frames):
        t_copy(lax.rem(f + step, frames)).start()
    own_w = pltpu.make_async_copy(w_ref, wg_ref.at[i], own_sem.at[0])
    own_n = pltpu.make_async_copy(n_ref, ng_ref.at[f], own_sem.at[1])
    own_t = pltpu.make_async_copy(t_ref.at[f], tg_ref.at[f], own_sem.at[2])
    own_w.start()
    own_n.start()
    own_t.start()

    def relay(step):
        from_left = i - 2 * step
        from_right = i + 2 * step

        @pl.when(p - step >= 0)
        def _():
            w_copy(w_ref, from_left, 0, mate).wait_recv()

            @pl.when(has_right)
            def _():
                w_copy(wg_ref.at[from_left], from_left, 0, right).start()

            w_copy(wg_ref.at[from_left], from_left, 2, mate).start()

        @pl.when(p + step <= line - 1)
        def _():
            w_copy(w_ref, from_right, 1, mate).wait_recv()

            @pl.when(has_left)
            def _():
                w_copy(wg_ref.at[from_right], from_right, 1, left).start()

            w_copy(wg_ref.at[from_right], from_right, 2, mate).start()

    def relay_norm():
        for step in range(1, pairs):
            far = lax.rem(u + step, pairs) * 2 + c
            n_copy(n_ref, far, 0, sibling).wait_recv()
            n_copy(ng_ref.at[far], far, 0, sibling).start()

    for step in range(1, min(line, 3)):
        relay(step)
    relay_norm()
    if line > 3:
        lax.fori_loop(3, line, lambda s, z: (relay(s), z)[1], 0)

    def finish(q, z):
        w_copy(w_ref, q * 2 + (1 - x), 2, mate).wait_recv()
        w_copy(w_ref, q * 2 + x, 2, mate).wait_send()

        @pl.when(jnp.logical_and(q <= p, has_right))
        def _():
            w_copy(w_ref, q * 2 + x, 0, right).wait_send()

        @pl.when(jnp.logical_and(q >= p, has_left))
        def _():
            w_copy(w_ref, q * 2 + x, 1, left).wait_send()

        return z

    for step in range(1, pairs):
        far = lax.rem(u + step, pairs) * 2 + c
        n_copy(n_ref, f, step, far).wait_send()
        n_copy(n_ref, far, 0, sibling).wait_send()
    n_copy(n_ref, f, 0, sibling).wait_send()
    for v in range(pairs):
        n_copy(n_ref, v * 2 + (1 - c), 0, sibling).wait_recv()
    for step in range(1, frames):
        other = lax.rem(f + step, frames)
        t_copy(other).wait_send()
        pltpu.make_async_remote_copy(
            src_ref=t_ref.at[other], dst_ref=tg_ref.at[other],
            send_sem=t_send.at[other], recv_sem=t_recv.at[other],
            device_id=(i, other), device_id_type=MESH,
        ).wait_recv()
    lax.fori_loop(0, line, finish, 0)
    own_w.wait()
    own_n.wait()
    own_t.wait()


def gather_all(dp, frames, weight, hidden, gain, bias, thinker):
    dma = pltpu.SemaphoreType.DMA
    any_spec = pl.BlockSpec(memory_space=pl.ANY)
    vmem = pl.BlockSpec(memory_space=pltpu.VMEM)
    pairs = frames // 2
    kinds, own_rows, head_cols = weight.shape
    think_rows = thinker.shape[0]
    w_own = (own_rows, kinds * head_cols)
    t_own = (frames, think_rows, head_cols)
    moved = 2 * (dp * weight.size + frames * hidden.size + thinker.size)
    return pl.pallas_call(
        functools.partial(gather_kernel, dp, frames),
        out_shape=(
            jax.ShapeDtypeStruct((dp,) + w_own, weight.dtype),
            jax.ShapeDtypeStruct((frames,) + hidden.shape, hidden.dtype),
            jax.ShapeDtypeStruct(t_own, thinker.dtype),
        ),
        in_specs=[vmem] * 5,
        out_specs=(any_spec,) * 3,
        scratch_shapes=[
            pltpu.VMEM(w_own, weight.dtype),
            pltpu.VMEM(hidden.shape, hidden.dtype),
            pltpu.VMEM(t_own, thinker.dtype),
            dma((3, dp)), dma((dp,)),
            dma((pairs, frames)), dma((frames,)),
            dma((frames,)), dma((frames,)),
            dma((3,)),
        ],
        compiler_params=pltpu.CompilerParams(
            collective_id=0, has_side_effects=True, vmem_limit_bytes=VMEM_LIMIT
        ),
        cost_estimate=pl.CostEstimate(flops=0, bytes_accessed=2 * moved, transcendentals=0),
        name="gather_all",
    )(weight, hidden, gain, bias, thinker)


def local_kernel(
    rows_tile, tile_q, windows, len_ref, pos_ref, n_ref, w_ref, t_ref, grad_s, nt_ref,
    q_s, k_s, v_s, g_s, kt_s, dq_s, dk_s, dv_s, dk_acc, dv_acc,
):
    length, width = n_ref.shape
    cols = w_ref.shape[1]
    heads = cols // (3 * HD)
    recs = len_ref.shape[1]
    slack = t_ref.shape[0] - length
    scale = HD ** (-0.5)
    expo_scale = scale * math.log2(math.e)

    ends = []
    total = 0
    for r in range(recs):
        total = total + len_ref[0, r]
        ends.append(total)

    @pl.loop(0, length // rows_tile)
    def _(t):
        r0 = pl.multiple_of(t * rows_tile, rows_tile)
        rows = pl.ds(r0, rows_tile)
        proj = jnp.dot(n_ref[rows, :], w_ref[...], preferred_element_type=jnp.float32)
        proj = proj.astype(jnp.bfloat16)
        frame_ids = r0 + lax.broadcasted_iota(jnp.int32, (rows_tile, HD), 0)
        lane = lax.broadcasted_iota(jnp.int32, (rows_tile, HD), 1)
        seg = jnp.zeros((rows_tile, HD), jnp.int32)
        for end in ends:
            seg = seg + jnp.where(frame_ids >= end, 1, 0)
        same = seg == lane
        q_mask = jnp.where(jnp.logical_or(same, lane >= recs), 0.0, NEG).astype(jnp.bfloat16)
        k_mask = jnp.where(same, 1.0, 0.0).astype(jnp.bfloat16)
        cover = rows_tile + slack
        col = r0 + lax.broadcasted_iota(jnp.int32, (rows_tile, cover), 1)
        places = jnp.broadcast_to(pos_ref[:, rows], (128, rows_tile)).T[:, 0:1]
        pick = jnp.where(col == places, 1.0, 0.0).astype(jnp.bfloat16)
        out_grad = jnp.dot(
            pick, t_ref[pl.ds(r0, cover), :], preferred_element_type=jnp.float32
        ).astype(jnp.bfloat16)
        for h in range(heads):
            base = 3 * HD * h
            keys = proj[:, base + HD:base + 2 * HD]
            q_s[h, rows, 0:HD] = proj[:, base:base + HD]
            q_s[h, rows, HD:2 * HD] = q_mask
            k_s[h, rows, 0:HD] = keys
            k_s[h, rows, HD:2 * HD] = k_mask
            kt_s[h, :, rows] = keys.T
            v_s[h, rows, :] = proj[:, base + 2 * HD:base + 3 * HD]
            g_s[h, rows, :] = out_grad[:, h * HD:(h + 1) * HD]

    tiles = length // tile_q
    nt = (((1,), (1,)), ((), ()))

    dk_acc[...] = jnp.zeros_like(dk_acc)
    dv_acc[...] = jnp.zeros_like(dv_acc)

    @pl.loop(0, tiles)
    def _(t):
        q0 = pl.multiple_of(t * tile_q, tile_q)
        q_last = q0 + tile_q - 1
        q_span = pl.ds(q0, tile_q)
        low = jnp.int32(0)
        high = jnp.int32(length)
        for end in ends:
            low = jnp.where(end <= q0, jnp.maximum(low, end), low)
            high = jnp.where(end > q_last, jnp.minimum(high, end), high)
        low = (low // 128) * 128
        need = high - low

        def attend(window):
            start = pl.multiple_of(jnp.minimum(low, length - window), 128)
            span = pl.ds(start, window)

            def products(h):
                scores = lax.dot_general(
                    k_s[h, span, :], q_s[h, q_span, :], nt, preferred_element_type=jnp.float32
                )
                grads = lax.dot_general(
                    v_s[h, span, :], g_s[h, q_span, :], nt, preferred_element_type=jnp.float32
                )
                return scores, grads

            def softmax_grads(scores, grads):
                top = jnp.max(scores, axis=0, keepdims=True)
                expo = jnp.exp2((scores - top) * expo_scale)
                weights = expo * (1.0 / jnp.sum(expo, axis=0, keepdims=True))
                row_dot = jnp.sum(weights * grads, axis=0, keepdims=True)
                score_grad = (weights * (grads - row_dot)).astype(jnp.bfloat16)
                return weights.astype(jnp.bfloat16), score_grad

            def accumulate(h, weights, score_grad):
                dv_acc[h, span, :] += jnp.dot(
                    weights, g_s[h, q_span, :], preferred_element_type=jnp.float32
                )
                dk_acc[h, span, :] += jnp.dot(
                    score_grad, q_s[h, q_span, 0:HD], preferred_element_type=jnp.float32
                )
                dq_t = jnp.dot(kt_s[h, :, span], score_grad, preferred_element_type=jnp.float32)
                dq_s[h, q_span, :] = (dq_t * scale).T.astype(jnp.bfloat16)

            nt_ref[:, q_span] = n_ref[q_span, :].T
            ahead = products(0)
            for h in range(heads):
                now = ahead
                if h + 1 < heads:
                    ahead = products(h + 1)
                accumulate(h, *softmax_grads(*now))

        smaller = 0
        for window in windows:
            @pl.when(jnp.logical_and(need > smaller, need <= window))
            def _(window=window):
                attend(window)
            smaller = window

    for h in range(heads):
        dk_s[h] = (dk_acc[h] * scale).astype(jnp.bfloat16)
        dv_s[h] = dv_acc[h].astype(jnp.bfloat16)

    @pl.loop(0, length // rows_tile)
    def _(t):
        rows = pl.ds(pl.multiple_of(t * rows_tile, rows_tile), rows_tile)
        parts = []
        for h in range(heads):
            parts += [dq_s[h, rows, :], dk_s[h, rows, :], dv_s[h, rows, :]]
        grad = jnp.concatenate(parts, axis=1)
        grad_s[rows, :] = grad


def local_work(lengths, positions, group_norm, weight, thinker):
    length, width = group_norm.shape
    cols = weight.shape[1]
    heads = cols // (3 * HD)
    rows_tile = 256
    tile_q = 256
    windows = tuple(w for w in (512, 768) if w < length) + (length,)
    vmem = pl.BlockSpec(memory_space=pltpu.VMEM)
    bf16, f32 = jnp.bfloat16, jnp.float32
    return pl.pallas_call(
        functools.partial(local_kernel, rows_tile, tile_q, windows),
        out_shape=(
            jax.ShapeDtypeStruct((length, cols), bf16),
            jax.ShapeDtypeStruct((width, length), bf16),
        ),
        in_specs=[pl.BlockSpec(memory_space=pltpu.SMEM)] + [vmem] * 4,
        out_specs=(vmem, vmem),
        scratch_shapes=[
            pltpu.VMEM((heads, length, 2 * HD), bf16),
            pltpu.VMEM((heads, length, 2 * HD), bf16),
            pltpu.VMEM((heads, length, HD), bf16),
            pltpu.VMEM((heads, length, HD), bf16),
            pltpu.VMEM((heads, HD, length), bf16),
            pltpu.VMEM((heads, length, HD), bf16),
            pltpu.VMEM((heads, length, HD), bf16),
            pltpu.VMEM((heads, length, HD), bf16),
            pltpu.VMEM((heads, length, HD), f32),
            pltpu.VMEM((heads, length, HD), f32),
        ],
        compiler_params=pltpu.CompilerParams(vmem_limit_bytes=VMEM_LIMIT),
        name="local_work",
    )(lengths, positions, group_norm, weight, thinker)


def reduce_kernel(
    dp, frames, nt_ref, grad_ref, w_hbm, h_ref, gain_ref, wout_ref, hout_ref,
    w_ref, wp_ref, np_ref, own_w, own_n, from_mate, from_line, to_line, from_sib, from_far, to_far,
    m_send, m_recv, l_send, l_recv, s_send, s_recv, f_send, f_recv, w_sem,
):
    line = dp // 2
    pairs = frames // 2
    i = lax.axis_index("dp")
    f = lax.axis_index("frame")
    x, p = lax.rem(i, 2), lax.div(i, 2)
    c, u = lax.rem(f, 2), lax.div(f, 2)
    mate = p * 2 + (1 - x)
    right, left = i + 2, i - 2
    has_right, has_left = p < line - 1, p > 0
    sibling = u * 2 + (1 - c)
    f32, bf16 = jnp.float32, jnp.bfloat16
    own_frames = h_ref.shape[0]

    load = pltpu.make_async_copy(w_hbm, w_ref, w_sem)
    load.start()

    def weight_block(slot):
        return jnp.dot(nt_ref[slot], grad_ref[...], preferred_element_type=f32).astype(bf16)

    def norm_block(owner):
        rows = pl.ds(pl.multiple_of(owner * own_frames, own_frames), own_frames)
        return lax.dot_general(
            grad_ref[rows, :], w_ref[...], (((1,), (1,)), ((), ())), preferred_element_type=f32
        ).astype(bf16)

    barrier = pltpu.get_barrier_semaphore()
    pl.semaphore_signal(barrier, inc=1, device_id=(mate, f), device_id_type=MESH)

    @pl.when(has_right)
    def _():
        pl.semaphore_signal(barrier, inc=1, device_id=(right, f), device_id_type=MESH)

    @pl.when(has_left)
    def _():
        pl.semaphore_signal(barrier, inc=1, device_id=(left, f), device_id_type=MESH)

    pl.semaphore_signal(barrier, inc=1, device_id=(i, sibling), device_id_type=MESH)
    for step in range(1, pairs):
        far = lax.rem(u + step, pairs) * 2 + c
        pl.semaphore_signal(barrier, inc=1, device_id=(i, far), device_id_type=MESH)
    ends = jnp.where(has_right, 1, 0) + jnp.where(has_left, 1, 0)
    pl.semaphore_wait(barrier, 1 + pairs + ends)

    def to_mate(q):
        return pltpu.make_async_remote_copy(
            src_ref=wp_ref.at[q], dst_ref=from_mate.at[q],
            send_sem=m_send.at[q], recv_sem=m_recv.at[q],
            device_id=(mate, f), device_id_type=MESH,
        )

    def along(q, way, target):
        return pltpu.make_async_remote_copy(
            src_ref=to_line.at[q], dst_ref=from_line.at[way, q],
            send_sem=l_send.at[q], recv_sem=l_recv.at[way, q],
            device_id=(target, f), device_id_type=MESH,
        )

    def to_sibling(v):
        return pltpu.make_async_remote_copy(
            src_ref=np_ref.at[v], dst_ref=from_sib.at[v],
            send_sem=s_send.at[v], recv_sem=s_recv.at[v],
            device_id=(i, sibling), device_id_type=MESH,
        )

    def to_other(v, slot):
        return pltpu.make_async_remote_copy(
            src_ref=to_far.at[v], dst_ref=from_far.at[slot],
            send_sem=f_send.at[v], recv_sem=f_recv.at[slot],
            device_id=(i, v * 2 + c), device_id_type=MESH,
        )

    ahead, behind = line - 1 - p, p

    def target_at(s):
        lower = jnp.where(s < ahead, line - 1 - s, s - ahead)
        upper = jnp.where(s < behind, s, line - 1 - (s - behind))
        return jnp.where(p < line // 2, lower, upper)

    def send_block(s, z):
        q = target_at(s)
        wp_ref[q] = weight_block(q * 2 + (1 - x))
        to_mate(q).start()
        return z

    def send_norm(v):
        np_ref[v] = norm_block(v * 2 + (1 - c))
        to_sibling(v).start()

    send_block(0, 0)
    load.wait()
    for step in range(1, pairs):
        send_norm(lax.rem(u + step, pairs))
    lax.fori_loop(1, line, send_block, 0)
    send_norm(u)
    for v in range(pairs):
        own_n[v] = norm_block(v * 2 + c)

    for step in range(1, pairs):
        v = lax.rem(u + step, pairs)
        to_sibling(v).wait_recv()
        to_far[v] = (own_n[v].astype(f32) + from_sib[v].astype(f32)).astype(bf16)
        to_other(v, u).start()

    def pass_on(s, z):
        q = target_at(s)
        own_w[q] = weight_block(q * 2 + x)
        to_mate(q).wait_recv()

        @pl.when(jnp.logical_and(q >= p, has_left))
        def _():
            along(q, 0, right).wait_recv()

        @pl.when(jnp.logical_and(q <= p, has_right))
        def _():
            along(q, 1, left).wait_recv()

        def own():
            return own_w[q].astype(f32) + from_mate[q].astype(f32)

        @pl.when(q > p)
        def _():
            @pl.when(has_left)
            def _():
                to_line[q] = (own() + from_line[0, q].astype(f32)).astype(bf16)

            @pl.when(jnp.logical_not(has_left))
            def _():
                to_line[q] = own().astype(bf16)

            along(q, 0, right).start()

        @pl.when(q < p)
        def _():
            @pl.when(has_right)
            def _():
                to_line[q] = (own() + from_line[1, q].astype(f32)).astype(bf16)

            @pl.when(jnp.logical_not(has_right))
            def _():
                to_line[q] = own().astype(bf16)

            along(q, 1, left).start()

        return z

    lax.fori_loop(0, line - 1, pass_on, 0)

    to_sibling(u).wait_recv()
    total = own_n[u].astype(f32) + from_sib[u].astype(f32)
    for step in range(1, pairs):
        v = lax.rem(u + step, pairs)
        to_other(v, v).wait_recv()
        total = total + from_far[v].astype(f32)
    rows = h_ref[...].astype(f32)
    mean_row = jnp.mean(rows, axis=-1, keepdims=True)
    centered = rows - mean_row
    inv_std = lax.rsqrt(jnp.mean(centered * centered, axis=-1, keepdims=True) + norm_eps)
    gain = gain_ref[...].reshape(1, -1)
    hout_ref[...] = norm_backward(total, centered * inv_std, inv_std, gain)

    pass_on(line - 1, 0)
    zero = jnp.zeros(wp_ref.shape[1:], f32)

    @pl.when(jnp.logical_not(has_left))
    def _():
        from_line[0, p] = zero.astype(bf16)

    @pl.when(jnp.logical_not(has_right))
    def _():
        from_line[1, p] = zero.astype(bf16)

    final = own_w[p].astype(f32) + from_mate[p].astype(f32)
    final = final + from_line[0, p].astype(f32) + from_line[1, p].astype(f32)
    wout_ref[...] = final

    def sent(q, z):
        to_mate(q).wait_send()

        @pl.when(q != p)
        def _():
            along(q, 0, right).wait_send()

        return z

    lax.fori_loop(0, line, sent, 0)
    for v in range(pairs):
        to_sibling(v).wait_send()
    for step in range(1, pairs):
        v = lax.rem(u + step, pairs)
        to_other(v, u).wait_send()


def reduce_all(dp, frames, norm_t, grad, weight, hidden, gain):
    dma = pltpu.SemaphoreType.DMA
    vmem = pl.BlockSpec(memory_space=pltpu.VMEM)
    pairs, line = frames // 2, dp // 2
    bf16, f32 = jnp.bfloat16, jnp.float32
    own_rows, cols = norm_t.shape[1], grad.shape[1]
    moved = 2 * (norm_t.size + weight.size)
    return pl.pallas_call(
        functools.partial(reduce_kernel, dp, frames),
        out_shape=(
            jax.ShapeDtypeStruct((own_rows, cols), f32),
            jax.ShapeDtypeStruct(hidden.shape, bf16),
        ),
        in_specs=[vmem] * 2 + [pl.BlockSpec(memory_space=pl.ANY)] + [vmem] * 2,
        out_specs=(vmem,) * 2,
        scratch_shapes=[
            pltpu.VMEM(weight.shape, bf16),
            pltpu.VMEM((line, own_rows, cols), bf16),
            pltpu.VMEM((pairs,) + hidden.shape, bf16),
            pltpu.VMEM((line, own_rows, cols), bf16),
            pltpu.VMEM((pairs,) + hidden.shape, bf16),
            pltpu.VMEM((line, own_rows, cols), bf16),
            pltpu.VMEM((2, line, own_rows, cols), bf16),
            pltpu.VMEM((line, own_rows, cols), bf16),
            pltpu.VMEM((pairs,) + hidden.shape, bf16),
            pltpu.VMEM((pairs,) + hidden.shape, bf16),
            pltpu.VMEM((pairs,) + hidden.shape, bf16),
            dma((line,)), dma((line,)), dma((line,)), dma((2, line)),
            dma((pairs,)), dma((pairs,)), dma((pairs,)), dma((pairs,)),
            dma,
        ],
        compiler_params=pltpu.CompilerParams(
            collective_id=1, has_side_effects=True, vmem_limit_bytes=VMEM_LIMIT
        ),
        cost_estimate=pl.CostEstimate(flops=0, bytes_accessed=2 * moved, transcendentals=0),
        name="reduce_all",
    )(norm_t, grad, weight, hidden, gain)


def finish_kernel(w_ref, h_ref, w_out, h_out):
    for h in range(w_out.shape[2] // HD):
        for kind in range(3):
            at = (3 * h + kind) * HD
            w_out[kind, :, h * HD:(h + 1) * HD] = w_ref[:, at:at + HD]
    h_out[...] = h_ref[...]


def finish(weight_grad, hidden_grad):
    vmem = pl.BlockSpec(memory_space=pltpu.VMEM)
    rows, cols = weight_grad.shape
    return pl.pallas_call(
        finish_kernel,
        out_shape=(
            jax.ShapeDtypeStruct((3, rows, cols // 3), jnp.float32),
            jax.ShapeDtypeStruct(hidden_grad.shape, hidden_grad.dtype),
        ),
        in_specs=[vmem] * 2,
        out_specs=(vmem,) * 2,
        name="finish",
    )(weight_grad, hidden_grad)


def per_device(
    hidden_in, rec_lengths, token_positions, thinker_grad, norm_gain, norm_bias, qkv_weight
):
    frame_count = lax.axis_size("frame")
    dp_count = lax.axis_size("dp")
    own_rows, three, head_cols = qkv_weight.shape
    heads = head_cols // HD
    own_frames, width = hidden_in.shape
    group_frames = token_positions.shape[0]
    think_rows = thinker_grad.shape[0]
    weight, group_norm, moved = gather_all(
        dp_count, frame_count, qkv_weight.transpose(1, 0, 2), hidden_in,
        norm_gain, norm_bias, thinker_grad,
    )
    weight = weight.reshape(width, 3 * head_cols)
    grad, norm_t = local_work(
        rec_lengths,
        token_positions.reshape(1, group_frames),
        group_norm.reshape(group_frames, width),
        weight,
        moved.reshape(frame_count * think_rows, head_cols),
    )
    weight_total, hidden_grad = reduce_all(
        dp_count, frame_count,
        norm_t.reshape(dp_count, own_rows, group_frames), grad, weight,
        hidden_in, norm_gain,
    )
    weight_grad, hidden_grad = finish(weight_total, hidden_grad)
    return (hidden_grad, weight_grad.transpose(1, 0, 2))


def solution(mesh):
    placed = (
        P(("dp", "frame"), None),
        P("dp", None),
        P("dp"),
        P(("dp", "frame"), None),
        P(),
        P(),
        P("dp", None, "frame"),
    )
    return jax.shard_map(
        per_device,
        mesh=mesh,
        in_specs=placed,
        out_specs=(P(("dp", "frame"), None), P("dp", None, "frame")),
        check_vma=False,
    )
```

```python
import functools
import math

import jax
import jax.numpy as jnp
from jax import lax
from jax.experimental import pallas as pl
from jax.experimental.pallas import tpu as pltpu
from jax.sharding import PartitionSpec as P

HD = 64
MESH = pl.DeviceIdType.MESH
VMEM_LIMIT = 56 * 1024 * 1024

norm_eps = 1e-05
NEG = -1e30


def norm_forward(rows, gain, bias):
    rows_f32 = rows.astype(jnp.float32)
    mean_row = jnp.mean(rows_f32, axis=-1, keepdims=True)
    centered = rows_f32 - mean_row
    variance = jnp.mean(centered * centered, axis=-1, keepdims=True)
    inv_std = lax.rsqrt(variance + norm_eps)
    standard = centered * inv_std
    normalized = (standard * gain + bias).astype(jnp.bfloat16)
    return (normalized, standard, inv_std)


def norm_backward(norm_grad, standard, inv_std, gain):
    scaled = norm_grad * gain
    result = inv_std * (
        scaled
        - jnp.mean(scaled, axis=-1, keepdims=True)
        - standard * jnp.mean(scaled * standard, axis=-1, keepdims=True)
    )
    return result.astype(jnp.bfloat16)


def gather_kernel(
    dp, frames, w_in, h_hbm, gain_ref, bias_ref, t_hbm, wg_ref, ng_ref, tg_ref,
    h_in, t_in, w_ref, n_ref, t_ref,
    w_send, w_recv, n_send, n_recv, t_send, t_recv, own_sem, in_sem,
):
    head_cols = w_in.shape[2]
    load_h = pltpu.make_async_copy(h_hbm, h_in, in_sem.at[0])
    load_t = pltpu.make_async_copy(t_hbm, t_in, in_sem.at[1])
    load_h.start()
    load_t.start()
    line = dp // 2
    pairs = frames // 2
    i = lax.axis_index("dp")
    f = lax.axis_index("frame")
    x, p = lax.rem(i, 2), lax.div(i, 2)
    c, u = lax.rem(f, 2), lax.div(f, 2)
    mate = p * 2 + (1 - x)
    right, left = i + 2, i - 2
    has_right, has_left = p < line - 1, p > 0

    barrier = pltpu.get_barrier_semaphore()
    pl.semaphore_signal(barrier, inc=1, device_id=(mate, f), device_id_type=MESH)

    @pl.when(has_right)
    def _():
        pl.semaphore_signal(barrier, inc=1, device_id=(right, f), device_id_type=MESH)

    @pl.when(has_left)
    def _():
        pl.semaphore_signal(barrier, inc=1, device_id=(left, f), device_id_type=MESH)

    for step in range(1, frames):
        other = lax.rem(f + step, frames)
        pl.semaphore_signal(barrier, inc=1, device_id=(i, other), device_id_type=MESH)
    for h in range(head_cols // HD):
        for kind in range(3):
            at = (3 * h + kind) * HD
            w_ref[:, at:at + HD] = w_in[kind, :, h * HD:(h + 1) * HD]

    ends = jnp.where(has_right, 1, 0) + jnp.where(has_left, 1, 0)
    pl.semaphore_wait(barrier, frames + ends)

    def w_copy(src, slot, way, target):
        return pltpu.make_async_remote_copy(
            src_ref=src, dst_ref=wg_ref.at[slot],
            send_sem=w_send.at[way, slot], recv_sem=w_recv.at[slot],
            device_id=(target, f), device_id_type=MESH,
        )

    def n_copy(src, slot, way, target):
        return pltpu.make_async_remote_copy(
            src_ref=src, dst_ref=ng_ref.at[slot],
            send_sem=n_send.at[way, slot], recv_sem=n_recv.at[slot],
            device_id=(i, target), device_id_type=MESH,
        )

    def t_copy(target):
        return pltpu.make_async_remote_copy(
            src_ref=t_ref.at[target], dst_ref=tg_ref.at[f],
            send_sem=t_send.at[target], recv_sem=t_recv.at[f],
            device_id=(i, target), device_id_type=MESH,
        )

    @pl.when(has_right)
    def _():
        w_copy(w_ref, i, 0, right).start()

    @pl.when(has_left)
    def _():
        w_copy(w_ref, i, 1, left).start()

    w_copy(w_ref, i, 2, mate).start()
    sibling = u * 2 + (1 - c)
    load_h.wait()
    n_ref[...] = norm_forward(
        h_in[...], gain_ref[...].reshape(1, -1), bias_ref[...].reshape(1, -1)
    )[0]
    for step in range(1, pairs):
        far = lax.rem(u + step, pairs) * 2 + c
        n_copy(n_ref, f, step, far).start()
    n_copy(n_ref, f, 0, sibling).start()
    load_t.wait()
    for target in range(frames):
        t_ref[target] = t_in[:, target * head_cols:(target + 1) * head_cols]
    for step in range(1, frames):
        t_copy(lax.rem(f + step, frames)).start()
    own_w = pltpu.make_async_copy(w_ref, wg_ref.at[i], own_sem.at[0])
    own_n = pltpu.make_async_copy(n_ref, ng_ref.at[f], own_sem.at[1])
    own_t = pltpu.make_async_copy(t_ref.at[f], tg_ref.at[f], own_sem.at[2])
    own_w.start()
    own_n.start()
    own_t.start()

    def relay(step):
        from_left = i - 2 * step
        from_right = i + 2 * step

        @pl.when(p - step >= 0)
        def _():
            w_copy(w_ref, from_left, 0, mate).wait_recv()

            @pl.when(has_right)
            def _():
                w_copy(wg_ref.at[from_left], from_left, 0, right).start()

            w_copy(wg_ref.at[from_left], from_left, 2, mate).start()

        @pl.when(p + step <= line - 1)
        def _():
            w_copy(w_ref, from_right, 1, mate).wait_recv()

            @pl.when(has_left)
            def _():
                w_copy(wg_ref.at[from_right], from_right, 1, left).start()

            w_copy(wg_ref.at[from_right], from_right, 2, mate).start()

    def relay_norm():
        for step in range(1, pairs):
            far = lax.rem(u + step, pairs) * 2 + c
            n_copy(n_ref, far, 0, sibling).wait_recv()
            n_copy(ng_ref.at[far], far, 0, sibling).start()

    for step in range(1, min(line, 3)):
        relay(step)
    relay_norm()
    if line > 3:
        lax.fori_loop(3, line, lambda s, z: (relay(s), z)[1], 0)

    def finish(q, z):
        w_copy(w_ref, q * 2 + (1 - x), 2, mate).wait_recv()
        w_copy(w_ref, q * 2 + x, 2, mate).wait_send()

        @pl.when(jnp.logical_and(q <= p, has_right))
        def _():
            w_copy(w_ref, q * 2 + x, 0, right).wait_send()

        @pl.when(jnp.logical_and(q >= p, has_left))
        def _():
            w_copy(w_ref, q * 2 + x, 1, left).wait_send()

        return z

    for step in range(1, pairs):
        far = lax.rem(u + step, pairs) * 2 + c
        n_copy(n_ref, f, step, far).wait_send()
        n_copy(n_ref, far, 0, sibling).wait_send()
    n_copy(n_ref, f, 0, sibling).wait_send()
    for v in range(pairs):
        n_copy(n_ref, v * 2 + (1 - c), 0, sibling).wait_recv()
    for step in range(1, frames):
        other = lax.rem(f + step, frames)
        t_copy(other).wait_send()
        pltpu.make_async_remote_copy(
            src_ref=t_ref.at[other], dst_ref=tg_ref.at[other],
            send_sem=t_send.at[other], recv_sem=t_recv.at[other],
            device_id=(i, other), device_id_type=MESH,
        ).wait_recv()
    lax.fori_loop(0, line, finish, 0)
    own_w.wait()
    own_n.wait()
    own_t.wait()


def gather_all(dp, frames, weight, hidden, gain, bias, thinker):
    dma = pltpu.SemaphoreType.DMA
    any_spec = pl.BlockSpec(memory_space=pl.ANY)
    vmem = pl.BlockSpec(memory_space=pltpu.VMEM)
    pairs = frames // 2
    kinds, own_rows, head_cols = weight.shape
    think_rows = thinker.shape[0]
    w_own = (own_rows, kinds * head_cols)
    t_own = (frames, think_rows, head_cols)
    moved = 2 * (dp * weight.size + frames * hidden.size + thinker.size)
    return pl.pallas_call(
        functools.partial(gather_kernel, dp, frames),
        out_shape=(
            jax.ShapeDtypeStruct((dp,) + w_own, weight.dtype),
            jax.ShapeDtypeStruct((frames,) + hidden.shape, hidden.dtype),
            jax.ShapeDtypeStruct(t_own, thinker.dtype),
        ),
        in_specs=[vmem, any_spec, vmem, vmem, any_spec],
        out_specs=(any_spec,) * 3,
        scratch_shapes=[
            pltpu.VMEM(hidden.shape, hidden.dtype),
            pltpu.VMEM(thinker.shape, thinker.dtype),
            pltpu.VMEM(w_own, weight.dtype),
            pltpu.VMEM(hidden.shape, hidden.dtype),
            pltpu.VMEM(t_own, thinker.dtype),
            dma((3, dp)), dma((dp,)),
            dma((pairs, frames)), dma((frames,)),
            dma((frames,)), dma((frames,)),
            dma((3,)), dma((2,)),
        ],
        compiler_params=pltpu.CompilerParams(
            collective_id=0, has_side_effects=True, vmem_limit_bytes=VMEM_LIMIT
        ),
        cost_estimate=pl.CostEstimate(flops=0, bytes_accessed=2 * moved, transcendentals=0),
        name="gather_all",
    )(weight, hidden, gain, bias, thinker)


def local_kernel(
    rows_tile, tile_q, windows, len_ref, pos_ref, n_ref, w_ref, t_ref, grad_s, nt_ref,
    q_s, k_s, v_s, g_s, kt_s, dq_s, dk_s, dv_s, dk_acc, dv_acc,
):
    length, width = n_ref.shape
    cols = w_ref.shape[1]
    heads = cols // (3 * HD)
    recs = len_ref.shape[1]
    slack = t_ref.shape[0] - length
    scale = HD ** (-0.5)
    expo_scale = scale * math.log2(math.e)

    ends = []
    total = 0
    for r in range(recs):
        total = total + len_ref[0, r]
        ends.append(total)

    @pl.loop(0, length // rows_tile)
    def _(t):
        r0 = pl.multiple_of(t * rows_tile, rows_tile)
        rows = pl.ds(r0, rows_tile)
        proj = jnp.dot(n_ref[rows, :], w_ref[...], preferred_element_type=jnp.float32)
        proj = proj.astype(jnp.bfloat16)
        frame_ids = r0 + lax.broadcasted_iota(jnp.int32, (rows_tile, HD), 0)
        lane = lax.broadcasted_iota(jnp.int32, (rows_tile, HD), 1)
        seg = jnp.zeros((rows_tile, HD), jnp.int32)
        for end in ends:
            seg = seg + jnp.where(frame_ids >= end, 1, 0)
        same = seg == lane
        q_mask = jnp.where(jnp.logical_or(same, lane >= recs), 0.0, NEG).astype(jnp.bfloat16)
        k_mask = jnp.where(same, 1.0, 0.0).astype(jnp.bfloat16)
        cover = rows_tile + slack
        col = r0 + lax.broadcasted_iota(jnp.int32, (rows_tile, cover), 1)
        places = jnp.broadcast_to(pos_ref[:, rows], (128, rows_tile)).T[:, 0:1]
        pick = jnp.where(col == places, 1.0, 0.0).astype(jnp.bfloat16)
        out_grad = jnp.dot(
            pick, t_ref[pl.ds(r0, cover), :], preferred_element_type=jnp.float32
        ).astype(jnp.bfloat16)
        for h in range(heads):
            base = 3 * HD * h
            keys = proj[:, base + HD:base + 2 * HD]
            q_s[h, rows, 0:HD] = proj[:, base:base + HD]
            q_s[h, rows, HD:2 * HD] = q_mask
            k_s[h, rows, 0:HD] = keys
            k_s[h, rows, HD:2 * HD] = k_mask
            kt_s[h, :, rows] = keys.T
            v_s[h, rows, :] = proj[:, base + 2 * HD:base + 3 * HD]
            g_s[h, rows, :] = out_grad[:, h * HD:(h + 1) * HD]

    tiles = length // tile_q
    nt = (((1,), (1,)), ((), ()))

    dk_acc[...] = jnp.zeros_like(dk_acc)
    dv_acc[...] = jnp.zeros_like(dv_acc)

    @pl.loop(0, tiles)
    def _(t):
        q0 = pl.multiple_of(t * tile_q, tile_q)
        q_last = q0 + tile_q - 1
        q_span = pl.ds(q0, tile_q)
        low = jnp.int32(0)
        high = jnp.int32(length)
        for end in ends:
            low = jnp.where(end <= q0, jnp.maximum(low, end), low)
            high = jnp.where(end > q_last, jnp.minimum(high, end), high)
        low = (low // 128) * 128
        need = high - low

        def attend(window):
            start = pl.multiple_of(jnp.minimum(low, length - window), 128)
            span = pl.ds(start, window)

            def products(h):
                scores = lax.dot_general(
                    k_s[h, span, :], q_s[h, q_span, :], nt, preferred_element_type=jnp.float32
                )
                grads = lax.dot_general(
                    v_s[h, span, :], g_s[h, q_span, :], nt, preferred_element_type=jnp.float32
                )
                return scores, grads

            def softmax_grads(scores, grads):
                top = jnp.max(scores, axis=0, keepdims=True)
                expo = jnp.exp2((scores - top) * expo_scale)
                weights = expo * (1.0 / jnp.sum(expo, axis=0, keepdims=True))
                row_dot = jnp.sum(weights * grads, axis=0, keepdims=True)
                score_grad = (weights * (grads - row_dot)).astype(jnp.bfloat16)
                return weights.astype(jnp.bfloat16), score_grad

            def accumulate(h, weights, score_grad):
                dv_acc[h, span, :] += jnp.dot(
                    weights, g_s[h, q_span, :], preferred_element_type=jnp.float32
                )
                dk_acc[h, span, :] += jnp.dot(
                    score_grad, q_s[h, q_span, 0:HD], preferred_element_type=jnp.float32
                )
                dq_t = jnp.dot(kt_s[h, :, span], score_grad, preferred_element_type=jnp.float32)
                dq_s[h, q_span, :] = (dq_t * scale).T.astype(jnp.bfloat16)

            nt_ref[:, q_span] = n_ref[q_span, :].T
            ahead = products(0)
            for h in range(heads):
                now = ahead
                if h + 1 < heads:
                    ahead = products(h + 1)
                accumulate(h, *softmax_grads(*now))

        smaller = 0
        for window in windows:
            @pl.when(jnp.logical_and(need > smaller, need <= window))
            def _(window=window):
                attend(window)
            smaller = window

    for h in range(heads):
        dk_s[h] = (dk_acc[h] * scale).astype(jnp.bfloat16)
        dv_s[h] = dv_acc[h].astype(jnp.bfloat16)

    @pl.loop(0, length // rows_tile)
    def _(t):
        rows = pl.ds(pl.multiple_of(t * rows_tile, rows_tile), rows_tile)
        parts = []
        for h in range(heads):
            parts += [dq_s[h, rows, :], dk_s[h, rows, :], dv_s[h, rows, :]]
        grad = jnp.concatenate(parts, axis=1)
        grad_s[rows, :] = grad


def local_work(lengths, positions, group_norm, weight, thinker):
    length, width = group_norm.shape
    cols = weight.shape[1]
    heads = cols // (3 * HD)
    rows_tile = 256
    tile_q = 256
    windows = tuple(w for w in (512, 640, 768, 896) if w < length) + (length,)
    vmem = pl.BlockSpec(memory_space=pltpu.VMEM)
    bf16, f32 = jnp.bfloat16, jnp.float32
    return pl.pallas_call(
        functools.partial(local_kernel, rows_tile, tile_q, windows),
        out_shape=(
            jax.ShapeDtypeStruct((length, cols), bf16),
            jax.ShapeDtypeStruct((width, length), bf16),
        ),
        in_specs=[pl.BlockSpec(memory_space=pltpu.SMEM)] + [vmem] * 4,
        out_specs=(vmem, vmem),
        scratch_shapes=[
            pltpu.VMEM((heads, length, 2 * HD), bf16),
            pltpu.VMEM((heads, length, 2 * HD), bf16),
            pltpu.VMEM((heads, length, HD), bf16),
            pltpu.VMEM((heads, length, HD), bf16),
            pltpu.VMEM((heads, HD, length), bf16),
            pltpu.VMEM((heads, length, HD), bf16),
            pltpu.VMEM((heads, length, HD), bf16),
            pltpu.VMEM((heads, length, HD), bf16),
            pltpu.VMEM((heads, length, HD), f32),
            pltpu.VMEM((heads, length, HD), f32),
        ],
        compiler_params=pltpu.CompilerParams(vmem_limit_bytes=VMEM_LIMIT),
        name="local_work",
    )(lengths, positions, group_norm, weight, thinker)


def reduce_kernel(
    dp, frames, nt_ref, grad_ref, w_hbm, h_ref, gain_ref, wout_ref, hout_ref,
    w_ref, wp_ref, np_ref, own_w, own_n, from_mate, from_line, to_line, from_sib, from_far, to_far,
    m_send, m_recv, l_send, l_recv, s_send, s_recv, f_send, f_recv, w_sem,
):
    line = dp // 2
    pairs = frames // 2
    i = lax.axis_index("dp")
    f = lax.axis_index("frame")
    x, p = lax.rem(i, 2), lax.div(i, 2)
    c, u = lax.rem(f, 2), lax.div(f, 2)
    mate = p * 2 + (1 - x)
    right, left = i + 2, i - 2
    has_right, has_left = p < line - 1, p > 0
    sibling = u * 2 + (1 - c)
    f32, bf16 = jnp.float32, jnp.bfloat16
    own_frames = h_ref.shape[0]

    load = pltpu.make_async_copy(w_hbm, w_ref, w_sem)
    load.start()

    def weight_block(slot):
        return jnp.dot(nt_ref[slot], grad_ref[...], preferred_element_type=f32).astype(bf16)

    def norm_block(owner):
        rows = pl.ds(pl.multiple_of(owner * own_frames, own_frames), own_frames)
        return lax.dot_general(
            grad_ref[rows, :], w_ref[...], (((1,), (1,)), ((), ())), preferred_element_type=f32
        ).astype(bf16)

    barrier = pltpu.get_barrier_semaphore()
    pl.semaphore_signal(barrier, inc=1, device_id=(mate, f), device_id_type=MESH)

    @pl.when(has_right)
    def _():
        pl.semaphore_signal(barrier, inc=1, device_id=(right, f), device_id_type=MESH)

    @pl.when(has_left)
    def _():
        pl.semaphore_signal(barrier, inc=1, device_id=(left, f), device_id_type=MESH)

    pl.semaphore_signal(barrier, inc=1, device_id=(i, sibling), device_id_type=MESH)
    for step in range(1, pairs):
        far = lax.rem(u + step, pairs) * 2 + c
        pl.semaphore_signal(barrier, inc=1, device_id=(i, far), device_id_type=MESH)
    ends = jnp.where(has_right, 1, 0) + jnp.where(has_left, 1, 0)
    pl.semaphore_wait(barrier, 1 + pairs + ends)

    def to_mate(q):
        return pltpu.make_async_remote_copy(
            src_ref=wp_ref.at[q], dst_ref=from_mate.at[q],
            send_sem=m_send.at[q], recv_sem=m_recv.at[q],
            device_id=(mate, f), device_id_type=MESH,
        )

    def along(q, way, target):
        return pltpu.make_async_remote_copy(
            src_ref=to_line.at[q], dst_ref=from_line.at[way, q],
            send_sem=l_send.at[q], recv_sem=l_recv.at[way, q],
            device_id=(target, f), device_id_type=MESH,
        )

    def to_sibling(v):
        return pltpu.make_async_remote_copy(
            src_ref=np_ref.at[v], dst_ref=from_sib.at[v],
            send_sem=s_send.at[v], recv_sem=s_recv.at[v],
            device_id=(i, sibling), device_id_type=MESH,
        )

    def to_other(v, slot):
        return pltpu.make_async_remote_copy(
            src_ref=to_far.at[v], dst_ref=from_far.at[slot],
            send_sem=f_send.at[v], recv_sem=f_recv.at[slot],
            device_id=(i, v * 2 + c), device_id_type=MESH,
        )

    ahead, behind = line - 1 - p, p

    def target_at(s):
        lower = jnp.where(s < ahead, line - 1 - s, s - ahead)
        upper = jnp.where(s < behind, s, line - 1 - (s - behind))
        return jnp.where(p < line // 2, lower, upper)

    def send_block(s, z):
        q = target_at(s)
        wp_ref[q] = weight_block(q * 2 + (1 - x))
        to_mate(q).start()
        return z

    def send_norm(v):
        np_ref[v] = norm_block(v * 2 + (1 - c))
        to_sibling(v).start()

    send_block(0, 0)
    load.wait()
    for step in range(1, pairs):
        send_norm(lax.rem(u + step, pairs))
    lax.fori_loop(1, line, send_block, 0)
    send_norm(u)
    for v in range(pairs):
        own_n[v] = norm_block(v * 2 + c)

    for step in range(1, pairs):
        v = lax.rem(u + step, pairs)
        to_sibling(v).wait_recv()
        to_far[v] = (own_n[v].astype(f32) + from_sib[v].astype(f32)).astype(bf16)
        to_other(v, u).start()

    def pass_on(s, z):
        q = target_at(s)
        own_w[q] = weight_block(q * 2 + x)
        to_mate(q).wait_recv()

        @pl.when(jnp.logical_and(q >= p, has_left))
        def _():
            along(q, 0, right).wait_recv()

        @pl.when(jnp.logical_and(q <= p, has_right))
        def _():
            along(q, 1, left).wait_recv()

        def own():
            return own_w[q].astype(f32) + from_mate[q].astype(f32)

        @pl.when(q > p)
        def _():
            @pl.when(has_left)
            def _():
                to_line[q] = (own() + from_line[0, q].astype(f32)).astype(bf16)

            @pl.when(jnp.logical_not(has_left))
            def _():
                to_line[q] = own().astype(bf16)

            along(q, 0, right).start()

        @pl.when(q < p)
        def _():
            @pl.when(has_right)
            def _():
                to_line[q] = (own() + from_line[1, q].astype(f32)).astype(bf16)

            @pl.when(jnp.logical_not(has_right))
            def _():
                to_line[q] = own().astype(bf16)

            along(q, 1, left).start()

        return z

    lax.fori_loop(0, line - 1, pass_on, 0)

    to_sibling(u).wait_recv()
    total = own_n[u].astype(f32) + from_sib[u].astype(f32)
    for step in range(1, pairs):
        v = lax.rem(u + step, pairs)
        to_other(v, v).wait_recv()
        total = total + from_far[v].astype(f32)
    rows = h_ref[...].astype(f32)
    mean_row = jnp.mean(rows, axis=-1, keepdims=True)
    centered = rows - mean_row
    inv_std = lax.rsqrt(jnp.mean(centered * centered, axis=-1, keepdims=True) + norm_eps)
    gain = gain_ref[...].reshape(1, -1)
    hout_ref[...] = norm_backward(total, centered * inv_std, inv_std, gain)

    pass_on(line - 1, 0)
    zero = jnp.zeros(wp_ref.shape[1:], f32)

    @pl.when(jnp.logical_not(has_left))
    def _():
        from_line[0, p] = zero.astype(bf16)

    @pl.when(jnp.logical_not(has_right))
    def _():
        from_line[1, p] = zero.astype(bf16)

    final = own_w[p].astype(f32) + from_mate[p].astype(f32)
    final = final + from_line[0, p].astype(f32) + from_line[1, p].astype(f32)
    wout_ref[...] = final

    def sent(q, z):
        to_mate(q).wait_send()

        @pl.when(q != p)
        def _():
            along(q, 0, right).wait_send()

        return z

    lax.fori_loop(0, line, sent, 0)
    for v in range(pairs):
        to_sibling(v).wait_send()
    for step in range(1, pairs):
        v = lax.rem(u + step, pairs)
        to_other(v, u).wait_send()


def reduce_all(dp, frames, norm_t, grad, weight, hidden, gain):
    dma = pltpu.SemaphoreType.DMA
    vmem = pl.BlockSpec(memory_space=pltpu.VMEM)
    pairs, line = frames // 2, dp // 2
    bf16, f32 = jnp.bfloat16, jnp.float32
    own_rows, cols = norm_t.shape[1], grad.shape[1]
    moved = 2 * (norm_t.size + weight.size)
    return pl.pallas_call(
        functools.partial(reduce_kernel, dp, frames),
        out_shape=(
            jax.ShapeDtypeStruct((own_rows, cols), f32),
            jax.ShapeDtypeStruct(hidden.shape, bf16),
        ),
        in_specs=[vmem] * 2 + [pl.BlockSpec(memory_space=pl.ANY)] + [vmem] * 2,
        out_specs=(vmem,) * 2,
        scratch_shapes=[
            pltpu.VMEM(weight.shape, bf16),
            pltpu.VMEM((line, own_rows, cols), bf16),
            pltpu.VMEM((pairs,) + hidden.shape, bf16),
            pltpu.VMEM((line, own_rows, cols), bf16),
            pltpu.VMEM((pairs,) + hidden.shape, bf16),
            pltpu.VMEM((line, own_rows, cols), bf16),
            pltpu.VMEM((2, line, own_rows, cols), bf16),
            pltpu.VMEM((line, own_rows, cols), bf16),
            pltpu.VMEM((pairs,) + hidden.shape, bf16),
            pltpu.VMEM((pairs,) + hidden.shape, bf16),
            pltpu.VMEM((pairs,) + hidden.shape, bf16),
            dma((line,)), dma((line,)), dma((line,)), dma((2, line)),
            dma((pairs,)), dma((pairs,)), dma((pairs,)), dma((pairs,)),
            dma,
        ],
        compiler_params=pltpu.CompilerParams(
            collective_id=1, has_side_effects=True, vmem_limit_bytes=VMEM_LIMIT
        ),
        cost_estimate=pl.CostEstimate(flops=0, bytes_accessed=2 * moved, transcendentals=0),
        name="reduce_all",
    )(norm_t, grad, weight, hidden, gain)


def finish_kernel(w_ref, h_ref, w_out, h_out):
    for h in range(w_out.shape[2] // HD):
        for kind in range(3):
            at = (3 * h + kind) * HD
            w_out[kind, :, h * HD:(h + 1) * HD] = w_ref[:, at:at + HD]
    h_out[...] = h_ref[...]


def finish(weight_grad, hidden_grad):
    vmem = pl.BlockSpec(memory_space=pltpu.VMEM)
    rows, cols = weight_grad.shape
    return pl.pallas_call(
        finish_kernel,
        out_shape=(
            jax.ShapeDtypeStruct((3, rows, cols // 3), jnp.float32),
            jax.ShapeDtypeStruct(hidden_grad.shape, hidden_grad.dtype),
        ),
        in_specs=[vmem] * 2,
        out_specs=(vmem,) * 2,
        name="finish",
    )(weight_grad, hidden_grad)


def per_device(
    hidden_in, rec_lengths, token_positions, thinker_grad, norm_gain, norm_bias, qkv_weight
):
    frame_count = lax.axis_size("frame")
    dp_count = lax.axis_size("dp")
    own_rows, three, head_cols = qkv_weight.shape
    heads = head_cols // HD
    own_frames, width = hidden_in.shape
    group_frames = token_positions.shape[0]
    think_rows = thinker_grad.shape[0]
    weight, group_norm, moved = gather_all(
        dp_count, frame_count, qkv_weight.transpose(1, 0, 2), hidden_in,
        norm_gain, norm_bias, thinker_grad,
    )
    weight = weight.reshape(width, 3 * head_cols)
    grad, norm_t = local_work(
        rec_lengths,
        token_positions.reshape(1, group_frames),
        group_norm.reshape(group_frames, width),
        weight,
        moved.reshape(frame_count * think_rows, head_cols),
    )
    weight_total, hidden_grad = reduce_all(
        dp_count, frame_count,
        norm_t.reshape(dp_count, own_rows, group_frames), grad, weight,
        hidden_in, norm_gain,
    )
    weight_grad, hidden_grad = finish(weight_total, hidden_grad)
    return (hidden_grad, weight_grad.transpose(1, 0, 2))


def solution(mesh):
    placed = (
        P(("dp", "frame"), None),
        P("dp", None),
        P("dp"),
        P(("dp", "frame"), None),
        P(),
        P(),
        P("dp", None, "frame"),
    )
    return jax.shard_map(
        per_device,
        mesh=mesh,
        in_specs=placed,
        out_specs=(P(("dp", "frame"), None), P("dp", None, "frame")),
        check_vma=False,
    )
```
